32 devices in a mesh: narrow: 4 (over z), wide: 8 (over y, x, core).
Axes of the slice: x: 2, y: 2, z: 4, core: 2. Of those that a mesh axis runs over, the one named last changes fastest.
Arguments:
- field: float32 [32, 128, 1024], P('narrow', 'wide'), may hold values from -12 to 12
- start_block: float32 [1024, 128], replicated, may hold values from -6 to 6
Outputs:
- mode2_gram: float32 [32, 32], P('narrow', 'wide')
The draws below stay inside these ranges and needn't reach their ends.
All inputs are finite; a program needn't handle non-finite values.
Results may differ from the reference program's by a relative error of at most 0.0001.
Values sent between devices are 32-bit elements; how exact they have to be, the bound alone decides.
No kernel may reach another device: no remote copies, remote signals or barrier semaphores. Data moves between devices by JAX's collectives and lax.ppermute only.
A program may use at most 64 MiB of HBM per device.

```python
import math
import jax
import jax.numpy as jnp
from jax import lax

I1 = 1024
RANK = 128
ITERS = 4
I2 = 32
I3 = 128


def draw_field(key, part):
    subkeys = jax.random.split(key, 8)
    noise_cells = jnp.clip(jax.random.normal(subkeys[0], (I2, I3, I1), jnp.float32), -4.0, 4.0)
    row_scale = jnp.exp(jax.random.uniform(subkeys[1], (1, 1, I1), jnp.float32, math.log(0.4), math.log(2.5)))
    middle_scale = jnp.exp(jax.random.uniform(subkeys[2], (I2, 1, 1), jnp.float32, math.log(0.6), math.log(1.6)))
    column_scale = jnp.exp(jax.random.uniform(subkeys[3], (1, I3, 1), jnp.float32, math.log(0.3), math.log(3.0)))
    mixing = jnp.eye(I1, dtype=jnp.float32) + 0.7 * jax.random.normal(subkeys[4], (I1, I1), jnp.float32) / math.sqrt(I1)
    mode_two_mix = jnp.eye(I2, dtype=jnp.float32) + jax.random.normal(subkeys[5], (I2, I2), jnp.float32) / math.sqrt(I2)
    scaled = noise_cells * row_scale * column_scale
    blended = jnp.dot(mode_two_mix, scaled.reshape(I2, I3 * I1), precision=lax.Precision.HIGHEST).reshape(I2, I3, I1)
    positions = jnp.arange(I2).astype(jnp.float32)
    phase = jax.random.uniform(subkeys[6], (), jnp.float32, 0.0, 2.0 * math.pi)
    profile = 1.0 + 0.5 * jnp.sin(4.0 * math.pi * positions / I2 + phase)
    shared = jnp.clip(jax.random.normal(subkeys[7], (1, I3, I1), jnp.float32), -4.0, 4.0) * row_scale * column_scale
    combined = (blended + 0.6 * profile.reshape(I2, 1, 1) * shared) * middle_scale
    mixed_field = jnp.dot(combined.reshape(I2 * I3, I1), mixing.T, precision=lax.Precision.HIGHEST)
    return jnp.clip(mixed_field.reshape(I2, I3, I1), -12.0, 12.0)


def centred(rng, extent, deviation, reach, held_as=jnp.bfloat16):
    array = deviation * jax.random.normal(rng, extent, jnp.float32)
    return jnp.clip(array, min=-reach, max=reach).astype(held_as)


def setup_inputs(seed: int = 0) -> dict:
    key_list = jax.random.split(jax.random.key(seed), 3)
    return {
        "field": draw_field(jax.random.fold_in(key_list[2], 71), 0),
        "start_block": centred(key_list[1], (I1, RANK), 1.0, 6.0, jnp.float32),
    }


def orthonormal(vectors):
    inner_gram = jnp.dot(vectors.T, vectors, precision=lax.Precision.HIGHEST)
    factor = jnp.linalg.cholesky(inner_gram)
    return jax.scipy.linalg.solve_triangular(factor, vectors.T, lower=True).T

def reference(field, start_block):
    unfolded = field.reshape(I2 * I3, I1)
    gram_one = jnp.dot(unfolded.T, unfolded, precision=lax.Precision.HIGHEST)
    subspace = orthonormal(start_block)
    for sweep_index in range(ITERS):
        subspace = orthonormal(jnp.dot(gram_one, subspace, precision=lax.Precision.HIGHEST))
    core_cells = jnp.dot(unfolded, subspace, precision=lax.Precision.HIGHEST)
    merged = core_cells.reshape(I2, I3 * RANK)
    product = jnp.dot(merged, merged.T, precision=lax.Precision.HIGHEST)
    return product / (RANK * I3)
```

```python
import functools
import jax
import jax.numpy as jnp
from jax import lax
from jax.experimental import pallas as pl
from jax.experimental.pallas import tpu as pltpu
from jax.sharding import PartitionSpec as P

ITERS = 4
BLOCK = 128
PANEL = 8
HIGHEST = lax.Precision.HIGHEST
NN = (((1,), (0,)), ((), ()))
NT = (((1,), (1,)), ((), ()))
SCALARS = pl.BlockSpec(memory_space=pltpu.SMEM)
VMEM = pl.BlockSpec(memory_space=pltpu.VMEM)


def split(values):
    high = values.astype(jnp.bfloat16)
    return high, (values - high.astype(jnp.float32)).astype(jnp.bfloat16)


def dot_bf16(left, right, dims):
    return lax.dot_general(left, right, dims, preferred_element_type=jnp.float32)


def dot_split(left, right, dims):
    (left_high, left_low), (right_high, right_low) = left, right
    return (
        dot_bf16(left_high, right_high, dims)
        + (dot_bf16(left_low, right_high, dims) + dot_bf16(left_high, right_low, dims))
    )


def dot_full(left, right, dims):
    return lax.dot_general(left, right, dims, precision=HIGHEST, preferred_element_type=jnp.float32)


def inverse_factor(matrix, out_ref):
    order = matrix.shape[0]
    panels = order // PANEL
    tiles = [matrix[PANEL * i : PANEL * (i + 1), :] for i in range(panels)]
    lane = lax.broadcasted_iota(jnp.int32, (PANEL, order), 1)

    def full(part):
        return jnp.broadcast_to(part, (PANEL, order))

    for p in range(panels):
        tile, start = tiles[p], PANEL * p
        inside = (lane >= start) & (lane < start + PANEL)
        columns = [full(tile[:, start + c : start + c + 1]) for c in range(PANEL)]
        pivot = {(r, c): full(columns[c][r : r + 1, :]) for c in range(PANEL) for r in range(c, PANEL)}
        rows = [
            jnp.where(inside, jnp.where(lane == start + c, 1.0, 0.0), full(tile[c : c + 1, :]))
            for c in range(PANEL)
        ]
        lower, inverse = {}, {}
        for c in range(PANEL):
            scale = lax.rsqrt(pivot[c, c])
            inverse[c, c] = scale
            for r in range(c + 1, PANEL):
                lower[r, c] = pivot[r, c] * scale
            for d in range(c + 1, PANEL):
                for r in range(d, PANEL):
                    pivot[r, d] = pivot[r, d] - lower[r, c] * lower[d, c]
        for c in range(PANEL):
            for r in range(c + 1, PANEL):
                total = lower[r, c] * inverse[c, c]
                for k in range(c + 1, r):
                    total = total + lower[r, k] * inverse[k, c]
                inverse[r, c] = -(inverse[r, r] * total)
        solved = []
        for r in range(PANEL):
            total = inverse[r, 0] * rows[0]
            for c in range(1, r + 1):
                total = total + inverse[r, c] * rows[c]
            solved.append(total)
            out_ref[start + r : start + r + 1, :] = jnp.where(lane < start + PANEL, total, 0.0)[0:1, :]
        if p == panels - 1:
            break
        eliminate = []
        for c in range(PANEL):
            total = inverse[PANEL - 1, c] * solved[PANEL - 1]
            for r in range(c, PANEL - 1):
                total = total + inverse[r, c] * solved[r]
            eliminate.append(total)
        for i in range(p + 1, panels):
            total = jnp.where(inside, 0.0, tiles[i])
            for c in range(PANEL):
                total = total - full(tiles[i][:, start + c : start + c + 1]) * eliminate[c]
            tiles[i] = total


def start_kernel(start_ref, out_ref, factor_ref):
    rows = start_ref[...].T
    inverse_factor(dot_full(rows, rows, NT), factor_ref)
    out_ref[...] = dot_full(factor_ref[...], rows, NN)


def gram_kernel(blocks, where_ref, own_ref, other_ref, *refs):
    outs, (high_ref, low_ref) = refs[:-2], refs[-2:]
    band = outs[0].shape[1]
    order = own_ref.shape[1]
    rows = own_ref.shape[0]
    for part, ref in enumerate((own_ref, other_ref)):
        high, low = split(ref[...])
        for target, values in ((high_ref, high), (low_ref, low)):
            target[rows * part : rows * (part + 1), 0:order] = values
            target[rows * part : rows * (part + 1), order : order + band - BLOCK] = values[:, : band - BLOCK]
    group, core = where_ref[0], where_ref[1]
    for k, out in enumerate(outs):
        first = pl.multiple_of((2 * jnp.bitwise_xor(group, k) + core) * BLOCK, BLOCK)
        left = [ref[:, pl.ds(first, BLOCK)].astype(jnp.float32).T.astype(jnp.bfloat16) for ref in (high_ref, low_ref)]
        right = [ref[:, pl.ds(first, band)] for ref in (high_ref, low_ref)]
        out[...] = dot_split(left, right, NN)


def cut_kernel(count, where_ref, *refs):
    terms, outs = refs[: len(refs) - count], refs[len(refs) - count :]
    rows = outs[0].shape[0]
    plane = where_ref[2]
    for k, out in enumerate(outs):
        piece = pl.ds(pl.multiple_of(jnp.bitwise_xor(plane, k) * rows, rows), rows)
        total = terms[0][piece, :]
        for term in terms[1:]:
            total = total + term[piece, :]
        out[...] = total


def add_kernel(*refs):
    total = refs[0][...]
    for term in refs[1:-1]:
        total = total + term[...]
    refs[-1][...] = total


def join_kernel(where_ref, *refs):
    pieces, out = refs[:-1], refs[-1]
    rows = pieces[0].shape[0]
    plane = where_ref[2]
    for k, piece in enumerate(pieces):
        out[pl.ds(pl.multiple_of(jnp.bitwise_xor(plane, k) * rows, rows), rows), :] = piece[...]


def sweep(basis, gram_high, gram_low, factor_ref):
    image = dot_split(split(basis), (gram_high, gram_low), NN)
    inverse_factor(dot_full(image, image, NT), factor_ref)
    return dot_full(factor_ref[...], image, NN)


def sweeps_and_core(basis_ref, field_ref, core_ref, high_ref, low_ref, factor_ref, basis_scratch):
    basis_scratch[...] = basis_ref[...]

    def body(step, carry):
        basis_scratch[...] = sweep(basis_scratch[...], high_ref[...], low_ref[...], factor_ref)
        return carry

    lax.fori_loop(0, ITERS, body, 0)
    core_ref[...] = dot_full(field_ref[...], basis_scratch[...], NT)


def banded_kernel(blocks, where_ref, basis_ref, field_ref, *refs):
    bands, (core_ref, high_ref, low_ref, factor_ref, basis_scratch) = refs[:-5], refs[-5:]
    group, core = where_ref[0], where_ref[1]
    half = len(bands) // 2
    for place, band in enumerate(bands):
        side = core if place < half else 1 - core
        row = 2 * jnp.bitwise_xor(group, place % half) + side
        rows = pl.ds(pl.multiple_of(row * BLOCK, BLOCK), BLOCK)
        for k in range(blocks // 2 + 1):
            column = lax.rem(row + k, blocks)
            columns = pl.ds(pl.multiple_of(column * BLOCK, BLOCK), BLOCK)
            part = band[:, BLOCK * k : BLOCK * (k + 1)]
            high_ref[rows, columns], low_ref[rows, columns] = split(part)
            if 0 < k < blocks // 2:
                high_ref[columns, rows], low_ref[columns, rows] = split(part.T)
    sweeps_and_core(basis_ref, field_ref, core_ref, high_ref, low_ref, factor_ref, basis_scratch)


def whole_kernel(basis_ref, field_ref, gram_ref, core_ref, high_ref, low_ref, factor_ref, basis_scratch):
    high_ref[...], low_ref[...] = split(gram_ref[...])
    sweeps_and_core(basis_ref, field_ref, core_ref, high_ref, low_ref, factor_ref, basis_scratch)


def pair_kernel(cells_three, where_ref, own_ref, *refs):
    cores, out_ref = refs[:-1], refs[-1]
    size = own_ref.shape[0]
    cells_two = size // cells_three
    row = lax.broadcasted_iota(jnp.int32, (size, size), 0)
    column = lax.broadcasted_iota(jnp.int32, (size, size), 1)
    same = lax.rem(row, cells_three) == lax.rem(column, cells_three)
    rows = jnp.where(
        lax.broadcasted_iota(jnp.int32, (cells_two, size), 0)
        == lax.broadcasted_iota(jnp.int32, (cells_two, size), 1) // cells_three,
        1.0,
        0.0,
    )
    width = out_ref.shape[1]
    target = lax.broadcasted_iota(jnp.int32, (size, width), 1)
    source = lax.broadcasted_iota(jnp.int32, (size, width), 0) // cells_three
    plane = where_ref[2]
    total = jnp.zeros(out_ref.shape, jnp.float32)
    for k, core in enumerate((own_ref, *cores)):
        product = jnp.where(same, dot_full(own_ref[...], core[...], NT), 0.0)
        place = jnp.where(target == source + jnp.bitwise_xor(plane, k) * cells_two, 1.0, 0.0)
        total = total + dot_full(dot_full(rows, product, NN), place, NN)
    out_ref[...] = total


def call(kernel, outs, name, operands, scratch=(), scalars=0, flops=0, limit=32):
    shapes = [jax.ShapeDtypeStruct(shape, jnp.float32) for shape in outs]
    touched = sum(operand.size for operand in operands) + sum(shape.size for shape in shapes)
    result = pl.pallas_call(
        kernel,
        out_shape=shapes,
        in_specs=[SCALARS] * scalars + [VMEM] * (len(operands) - scalars),
        out_specs=[VMEM] * len(shapes),
        scratch_shapes=list(scratch),
        compiler_params=pltpu.CompilerParams(vmem_limit_bytes=limit * 2**20),
        cost_estimate=pl.CostEstimate(flops=flops, bytes_accessed=4 * touched, transcendentals=0),
        name=name,
    )(*operands)
    return result if len(outs) > 1 else result[0]


def swap(array, axis, mask):
    return lax.ppermute(array, axis, [(i, i ^ mask) for i in range(lax.axis_size(axis))])


def shards(field, start_block):
    cells_two, cells_three, order = field.shape
    rank = start_block.shape[1]
    narrow, wide = lax.axis_size("narrow"), lax.axis_size("wide")
    unfolded = field.reshape(cells_two * cells_three, order)
    cells = unfolded.shape[0]
    place, plane = lax.axis_index("wide"), lax.axis_index("narrow")
    where = jnp.stack([place // 2, place % 2, plane]).astype(jnp.int32)
    basis = call(
        start_kernel, [(rank, order)], "orth_start", [start_block], [pltpu.VMEM((rank, rank), jnp.float32)], flops=10**9
    )
    scratch = [
        pltpu.VMEM((order, order), jnp.bfloat16),
        pltpu.VMEM((order, order), jnp.bfloat16),
        pltpu.VMEM((rank, rank), jnp.float32),
        pltpu.VMEM((rank, order), jnp.float32),
    ]
    blocks = order // BLOCK
    if wide == blocks and narrow & (narrow - 1) == 0 and BLOCK % (8 * narrow) == 0:
        groups = wide // 2
        band = BLOCK * (blocks // 2 + 1)
        other = swap(unfolded, "wide", 1)
        parts = call(
            functools.partial(gram_kernel, blocks),
            [(BLOCK, band)] * groups,
            "gram_band",
            [where, unfolded, other],
            [pltpu.VMEM((2 * cells, order + band - BLOCK), jnp.bfloat16)] * 2,
            scalars=1,
        )
        arrived = [swap(parts[k], "wide", 2 * k) for k in range(1, groups)]
        cuts = call(
            functools.partial(cut_kernel, narrow),
            [(BLOCK // narrow, band)] * narrow,
            "sum_groups",
            [where, parts[0], *arrived],
            scalars=1,
        )
        arrived = [swap(cuts[k], "narrow", k) for k in range(1, narrow)]
        piece = call(add_kernel, [(BLOCK // narrow, band)], "sum_planes", [cuts[0], *arrived])
        arrived = [swap(piece, "narrow", k) for k in range(1, narrow)]
        joined = call(join_kernel, [(BLOCK, band)], "join_planes", [where, piece, *arrived], scalars=1)
        bands = [joined] + [swap(joined, "wide", 2 * k) for k in range(1, groups)]
        bands = bands + [swap(part, "wide", 1) for part in bands]
        core = call(
            functools.partial(banded_kernel, blocks),
            [(cells, rank)],
            "sweeps",
            [where, basis, unfolded, *bands],
            scratch,
            scalars=1,
        )
    else:
        gram = lax.psum(lax.dot_general(unfolded, unfolded, (((0,), (0,)), ((), ())), precision=HIGHEST), ("narrow", "wide"))
        core = call(whole_kernel, [(cells, rank)], "sweeps", [basis, unfolded, gram], scratch)
    if narrow & (narrow - 1) == 0 and wide & (wide - 1) == 0:
        cores = [swap(core, "narrow", k) for k in range(1, narrow)]
        width = -(-narrow * cells_two // BLOCK) * BLOCK
        total = call(
            functools.partial(pair_kernel, cells_three),
            [(cells_two, width)],
            "pair_gram",
            [where, core, *cores],
            scalars=1,
        )
        mask = 1
        while mask < wide:
            total = total + swap(total, "wide", mask)
            mask *= 2
        columns = narrow * cells_two // wide
        finished = lax.dynamic_slice_in_dim(total, place * columns, columns, 1)
    else:
        merged = core.reshape(cells_two, cells_three * rank)
        everyone = lax.all_gather(merged, "narrow", axis=0, tiled=True)
        part = lax.dot_general(merged, everyone, NT, precision=HIGHEST)
        finished = lax.psum_scatter(part, "wide", scatter_dimension=1, tiled=True)
    return finished / (rank * cells_three * wide)


def solution(mesh):
    return jax.shard_map(
        shards,
        mesh=mesh,
        in_specs=(P("narrow", "wide", None), P()),
        out_specs=P("narrow", "wide"),
        check_vma=False,
    )
```

```python
import functools
import jax
import jax.numpy as jnp
from jax import lax
from jax.experimental import pallas as pl
from jax.experimental.pallas import tpu as pltpu
from jax.sharding import PartitionSpec as P

ITERS = 4
BLOCK = 128
PANEL = 8
HIGHEST = lax.Precision.HIGHEST
NN = (((1,), (0,)), ((), ()))
NT = (((1,), (1,)), ((), ()))
SCALARS = pl.BlockSpec(memory_space=pltpu.SMEM)
VMEM = pl.BlockSpec(memory_space=pltpu.VMEM)


def split(values):
    high = values.astype(jnp.bfloat16)
    return high, (values - high.astype(jnp.float32)).astype(jnp.bfloat16)


def dot_bf16(left, right, dims):
    return lax.dot_general(left, right, dims, preferred_element_type=jnp.float32)


def dot_split(left, right, dims):
    (left_high, left_low), (right_high, right_low) = left, right
    return (
        dot_bf16(left_high, right_high, dims)
        + (dot_bf16(left_low, right_high, dims) + dot_bf16(left_high, right_low, dims))
    )


def dot_full(left, right, dims):
    return lax.dot_general(left, right, dims, precision=HIGHEST, preferred_element_type=jnp.float32)


def add_pairs(terms):
    terms = list(terms)
    while len(terms) > 1:
        pairs = [terms[i] + terms[i + 1] for i in range(0, len(terms) - 1, 2)]
        terms = pairs + terms[2 * len(pairs) :]
    return terms[0]


def inverse_factor(matrix, out_ref, scratch):
    order = matrix.shape[0]
    panels = order // PANEL
    tiles = [matrix[PANEL * i : PANEL * (i + 1), :] for i in range(panels)]
    lane = lax.broadcasted_iota(jnp.int32, (PANEL, order), 1)

    def full(part):
        return jnp.broadcast_to(part, (PANEL, order))

    for p in range(panels):
        tile, start = tiles[p], PANEL * p
        base = PANEL * PANEL * (p % 2)
        inside = (lane >= start) & (lane < start + PANEL)
        for c in range(PANEL):
            scratch[base + PANEL * c : base + PANEL * (c + 1), :] = full(tile[:, start + c : start + c + 1])
        pivot = {
            (r, c): full(scratch[base + PANEL * c + r : base + PANEL * c + r + 1, :])
            for c in range(PANEL)
            for r in range(c, PANEL)
        }
        rows = [
            jnp.where(inside, jnp.where(lane == start + c, 1.0, 0.0), full(tile[c : c + 1, :]))
            for c in range(PANEL)
        ]
        reciprocal, inverse = {}, {}
        for c in range(PANEL):
            reciprocal[c] = 1.0 / pivot[c, c]
            lower = {r: pivot[r, c] * reciprocal[c] for r in range(c + 1, PANEL)}
            for d in range(c + 1, PANEL):
                for r in range(d, PANEL):
                    if r == c + 1:
                        pivot[r, d] = pivot[r, d] - (pivot[r, c] * pivot[d, c]) * reciprocal[c]
                    else:
                        pivot[r, d] = pivot[r, d] - lower[r] * pivot[d, c]
            for r in range(c + 1, PANEL):
                rows[r] = rows[r] - lower[r] * rows[c]
                for k in range(c):
                    inverse[r, k] = inverse[r, k] - lower[r] * inverse[c, k]
                inverse[r, c] = -lower[r]
        for r in range(PANEL):
            done = jnp.where(lane < start + PANEL, rows[r], 0.0) * lax.rsqrt(pivot[r, r])
            out_ref[start + r : start + r + 1, :] = done[0:1, :]
        if p == panels - 1:
            break
        scaled = [rows[r] * reciprocal[r] for r in range(PANEL)]
        eliminate = []
        for c in range(PANEL):
            total = scaled[c]
            for r in range(c + 1, PANEL):
                total = total + inverse[r, c] * scaled[r]
            eliminate.append(total)
        for i in range(p + 1, panels):
            steps = [full(tiles[i][:, start + c : start + c + 1]) * eliminate[c] for c in range(PANEL)]
            tiles[i] = jnp.where(inside, 0.0, tiles[i]) - add_pairs(steps)


def start_kernel(after_ref, start_ref, out_ref, factor_ref, spread_ref):
    del after_ref
    rows = start_ref[...].T
    inverse_factor(dot_full(rows, rows, NT), factor_ref, spread_ref)
    out_ref[...] = dot_full(factor_ref[...], rows, NN)


def split_kernel(rows_ref, high_ref, low_ref):
    order = rows_ref.shape[1]
    extra = high_ref.shape[1] - order
    for target, values in zip((high_ref, low_ref), split(rows_ref[...])):
        target[:, 0:order] = values
        target[:, order : order + extra] = values[:, :extra]


def gram_kernel(where_ref, own_high, own_low, other_ref, *refs):
    outs, (high_ref, low_ref) = refs[:-2], refs[-2:]
    band = outs[0].shape[1]
    rows, order = other_ref.shape
    extra = high_ref.shape[1] - order
    for own, target, values in zip((own_high, own_low), (high_ref, low_ref), split(other_ref[...])):
        target[0:rows, :] = own[...]
        target[rows : 2 * rows, 0:order] = values
        target[rows : 2 * rows, order : order + extra] = values[:, :extra]
    group, core = where_ref[0], where_ref[1]
    for k, out in enumerate(outs):
        first = pl.multiple_of((2 * jnp.bitwise_xor(group, k) + core) * BLOCK, BLOCK)
        left = [ref[:, pl.ds(first, BLOCK)].astype(jnp.float32).T.astype(jnp.bfloat16) for ref in (high_ref, low_ref)]
        right = [ref[:, pl.ds(first, band)] for ref in (high_ref, low_ref)]
        out[...] = dot_split(left, right, NN)


def cut_kernel(count, where_ref, after_ref, *refs):
    del after_ref
    terms, outs = refs[: len(refs) - count], refs[len(refs) - count :]
    rows = outs[0].shape[0]
    plane = where_ref[2]
    for k, out in enumerate(outs):
        piece = pl.ds(pl.multiple_of(jnp.bitwise_xor(plane, k) * rows, rows), rows)
        total = terms[0][piece, :]
        for term in terms[1:]:
            total = total + term[piece, :]
        out[...] = total


def add_kernel(*refs):
    total = refs[0][...]
    for term in refs[1:-1]:
        total = total + term[...]
    refs[-1][...] = total


def join_kernel(where_ref, *refs):
    pieces, out = refs[:-1], refs[-1]
    rows = pieces[0].shape[0]
    plane = where_ref[2]
    for k, piece in enumerate(pieces):
        out[pl.ds(pl.multiple_of(jnp.bitwise_xor(plane, k) * rows, rows), rows), :] = piece[...]


def sweeps_and_core(basis_ref, field_ref, core_ref, last_ref, high_ref, low_ref, factor_ref, spread_ref, image_ref):
    def times_gram(rows):
        return dot_split(split(rows), (high_ref[...], low_ref[...]), NN)

    def body(step, carry):
        image = image_ref[...]
        halves = split(image)
        inner = dot_split(halves, halves, NT)
        following = times_gram(image)
        inverse_factor(inner, factor_ref, spread_ref)
        image_ref[...] = dot_split(split(factor_ref[...]), split(following), NN)
        return carry

    image_ref[...] = times_gram(basis_ref[...])
    lax.fori_loop(0, ITERS - 1, body, 0)
    image = image_ref[...]
    last_ref[...] = dot_full(image, image, NT)
    core_ref[...] = dot_full(field_ref[...], image, NT)


def last_kernel(matrix_ref, out_ref, spread_ref):
    inverse_factor(matrix_ref[...], out_ref, spread_ref)


def banded_kernel(blocks, where_ref, basis_ref, field_ref, *refs):
    bands, rest = refs[:-7], refs[-7:]
    high_ref, low_ref = rest[2:4]
    group, core = where_ref[0], where_ref[1]
    half = len(bands) // 2
    for place, band in enumerate(bands):
        side = core if place < half else 1 - core
        row = 2 * jnp.bitwise_xor(group, place % half) + side
        rows = pl.ds(pl.multiple_of(row * BLOCK, BLOCK), BLOCK)
        for k in range(blocks // 2 + 1):
            column = lax.rem(row + k, blocks)
            columns = pl.ds(pl.multiple_of(column * BLOCK, BLOCK), BLOCK)
            part = band[:, BLOCK * k : BLOCK * (k + 1)]
            high_ref[rows, columns], low_ref[rows, columns] = split(part)
            if 0 < k < blocks // 2:
                high_ref[columns, rows], low_ref[columns, rows] = split(part.T)
    sweeps_and_core(basis_ref, field_ref, *rest)


def whole_kernel(basis_ref, field_ref, gram_ref, *rest):
    rest[2][...], rest[3][...] = split(gram_ref[...])
    sweeps_and_core(basis_ref, field_ref, *rest)


def pair_kernel(cells_three, where_ref, factor_ref, *refs):
    images, out_ref = refs[:-1], refs[-1]
    size = images[0].shape[0]
    cells_two = size // cells_three
    cores = [dot_full(image[...], factor_ref[...], NT) for image in images]
    row = lax.broadcasted_iota(jnp.int32, (size, size), 0)
    column = lax.broadcasted_iota(jnp.int32, (size, size), 1)
    same = lax.rem(row, cells_three) == lax.rem(column, cells_three)
    width = out_ref.shape[1]
    target = lax.broadcasted_iota(jnp.int32, (size, width), 1)
    source = lax.broadcasted_iota(jnp.int32, (size, width), 0) // cells_three
    plane = where_ref[2]
    total = jnp.zeros(out_ref.shape, jnp.float32)
    for k, core in enumerate(cores):
        product = jnp.where(same, dot_full(cores[0], core, NT), 0.0)
        summed = jnp.sum(product.reshape(cells_two, cells_three, size), axis=1)
        place = jnp.where(target == source + jnp.bitwise_xor(plane, k) * cells_two, 1.0, 0.0)
        total = total + dot_full(summed, place, NN)
    out_ref[...] = total


def call(kernel, outs, name, operands, scratch=(), scalars=0, order_only=(), flops=0, dtype=jnp.float32):
    shapes = [jax.ShapeDtypeStruct(shape, dtype) for shape in outs]
    touched = sum(operand.size for operand in operands) + sum(shape.size for shape in shapes)
    result = pl.pallas_call(
        kernel,
        out_shape=shapes,
        in_specs=[SCALARS] * scalars
        + [pl.BlockSpec(memory_space=pl.ANY)] * len(order_only)
        + [VMEM] * (len(operands) - scalars),
        out_specs=[VMEM] * len(shapes),
        scratch_shapes=list(scratch),
        compiler_params=pltpu.CompilerParams(vmem_limit_bytes=32 * 2**20),
        cost_estimate=pl.CostEstimate(flops=flops, bytes_accessed=4 * touched, transcendentals=0),
        name=name,
    )(*operands[:scalars], *order_only, *operands[scalars:])
    return result if len(outs) > 1 else result[0]


def swap(array, axis, mask):
    return lax.ppermute(array, axis, [(i, i ^ mask) for i in range(lax.axis_size(axis))])


def shards(field, start_block):
    cells_two, cells_three, order = field.shape
    rank = start_block.shape[1]
    narrow, wide = lax.axis_size("narrow"), lax.axis_size("wide")
    unfolded = field.reshape(cells_two * cells_three, order)
    cells = unfolded.shape[0]
    place, plane = lax.axis_index("wide"), lax.axis_index("narrow")
    where = jnp.stack([place // 2, place % 2, plane]).astype(jnp.int32)
    spread = pltpu.VMEM((2 * PANEL * PANEL, rank), jnp.float32)

    def orthonormal_start(after):
        return call(
            start_kernel,
            [(rank, order)],
            "orth_start",
            [start_block],
            [pltpu.VMEM((rank, rank), jnp.float32), spread],
            order_only=[after],
            flops=10**9,
        )

    scratch = [
        pltpu.VMEM((order, order), jnp.bfloat16),
        pltpu.VMEM((order, order), jnp.bfloat16),
        pltpu.VMEM((rank, rank), jnp.float32),
        spread,
        pltpu.VMEM((rank, order), jnp.float32),
    ]
    results = [(cells, rank), (rank, rank)]
    blocks = order // BLOCK
    if wide == blocks and narrow & (narrow - 1) == 0 and BLOCK % (8 * narrow) == 0:
        groups = wide // 2
        band = BLOCK * (blocks // 2 + 1)
        extended = (cells, order + band - BLOCK)
        other = swap(unfolded, "wide", 1)
        own = call(split_kernel, [extended] * 2, "split_field", [unfolded], dtype=jnp.bfloat16)
        parts = call(
            gram_kernel,
            [(BLOCK, band)] * groups,
            "gram_band",
            [where, *own, other],
            [pltpu.VMEM((2 * cells, extended[1]), jnp.bfloat16)] * 2,
            scalars=1,
        )
        arrived = [swap(parts[k], "wide", 2 * k) for k in range(1, groups)]
        basis = orthonormal_start(parts[0])
        cuts = call(
            functools.partial(cut_kernel, narrow),
            [(BLOCK // narrow, band)] * narrow,
            "sum_groups",
            [where, parts[0], *arrived],
            scalars=1,
            order_only=[basis],
        )
        arrived = [swap(cuts[k], "narrow", k) for k in range(1, narrow)]
        piece = call(add_kernel, [(BLOCK // narrow, band)], "sum_planes", [cuts[0], *arrived])
        arrived = [swap(piece, "narrow", k) for k in range(1, narrow)]
        joined = call(join_kernel, [(BLOCK, band)], "join_planes", [where, piece, *arrived], scalars=1)
        bands = [joined] + [swap(joined, "wide", 2 * k) for k in range(1, groups)]
        bands = bands + [swap(part, "wide", 1) for part in bands]
        image, inner = call(
            functools.partial(banded_kernel, blocks),
            results,
            "sweeps",
            [where, basis, unfolded, *bands],
            scratch,
            scalars=1,
        )
    else:
        basis = orthonormal_start(start_block)
        gram = lax.dot_general(unfolded, unfolded, (((0,), (0,)), ((), ())), precision=HIGHEST)
        gram = lax.psum(gram, ("narrow", "wide"))
        image, inner = call(whole_kernel, results, "sweeps", [basis, unfolded, gram], scratch)
    factor = call(last_kernel, [(rank, rank)], "last_factor", [inner], [spread], flops=10**9)
    if narrow & (narrow - 1) == 0 and wide & (wide - 1) == 0:
        images = [image] + [swap(image, "narrow", k) for k in range(1, narrow)]
        width = -(-narrow * cells_two // BLOCK) * BLOCK
        total = call(
            functools.partial(pair_kernel, cells_three),
            [(cells_two, width)],
            "pair_gram",
            [where, factor, *images],
            scalars=1,
        )
        mask = 1
        while mask < wide:
            total = total + swap(total, "wide", mask)
            mask *= 2
        columns = narrow * cells_two // wide
        finished = lax.dynamic_slice_in_dim(total, place * columns, columns, 1)
    else:
        core = lax.dot_general(image, factor, NT, precision=HIGHEST)
        merged = core.reshape(cells_two, cells_three * rank)
        everyone = lax.all_gather(merged, "narrow", axis=0, tiled=True)
        part = lax.dot_general(merged, everyone, NT, precision=HIGHEST)
        finished = lax.psum_scatter(part, "wide", scatter_dimension=1, tiled=True)
    return finished / (rank * cells_three * wide)


def solution(mesh):
    return jax.shard_map(
        shards,
        mesh=mesh,
        in_specs=(P("narrow", "wide", None), P()),
        out_specs=P("narrow", "wide"),
        check_vma=False,
    )
```

```python
import functools
import jax
import jax.numpy as jnp
from jax import lax
from jax.experimental import pallas as pl
from jax.experimental.pallas import tpu as pltpu
from jax.sharding import PartitionSpec as P

ITERS = 4
BLOCK = 128
PANEL = 8
HIGHEST = lax.Precision.HIGHEST
NN = (((1,), (0,)), ((), ()))
NT = (((1,), (1,)), ((), ()))
SCALARS = pl.BlockSpec(memory_space=pltpu.SMEM)
VMEM = pl.BlockSpec(memory_space=pltpu.VMEM)


def split(values):
    high = values.astype(jnp.bfloat16)
    return high, (values - high.astype(jnp.float32)).astype(jnp.bfloat16)


def dot_bf16(left, right, dims):
    return lax.dot_general(left, right, dims, preferred_element_type=jnp.float32)


def dot_split(left, right, dims):
    (left_high, left_low), (right_high, right_low) = left, right
    return (
        dot_bf16(left_high, right_high, dims)
        + (dot_bf16(left_low, right_high, dims) + dot_bf16(left_high, right_low, dims))
    )


def dot_full(left, right, dims):
    return lax.dot_general(left, right, dims, precision=HIGHEST, preferred_element_type=jnp.float32)


def add_pairs(terms):
    terms = list(terms)
    while len(terms) > 1:
        pairs = [terms[i] + terms[i + 1] for i in range(0, len(terms) - 1, 2)]
        terms = pairs + terms[2 * len(pairs) :]
    return terms[0]


def inverse_factor(matrix, out_ref, scratch):
    order = matrix.shape[0]
    panels = order // PANEL
    tiles = [matrix[PANEL * i : PANEL * (i + 1), :] for i in range(panels)]
    lane = lax.broadcasted_iota(jnp.int32, (PANEL, order), 1)

    def full(part):
        return jnp.broadcast_to(part, (PANEL, order))

    for p in range(panels):
        tile, start = tiles[p], PANEL * p
        base = PANEL * PANEL * (p % 2)
        inside = (lane >= start) & (lane < start + PANEL)
        for c in range(PANEL):
            scratch[base + PANEL * c : base + PANEL * (c + 1), :] = full(tile[:, start + c : start + c + 1])
        pivot = {
            (r, c): full(scratch[base + PANEL * c + r : base + PANEL * c + r + 1, :])
            for c in range(PANEL)
            for r in range(c, PANEL)
        }
        rows = [
            jnp.where(inside, jnp.where(lane == start + c, 1.0, 0.0), full(tile[c : c + 1, :]))
            for c in range(PANEL)
        ]
        reciprocal, inverse = {}, {}
        for c in range(PANEL):
            reciprocal[c] = 1.0 / pivot[c, c]
            lower = {r: pivot[r, c] * reciprocal[c] for r in range(c + 1, PANEL)}
            for d in range(c + 1, PANEL):
                for r in range(d, PANEL):
                    if r == c + 1:
                        pivot[r, d] = pivot[r, d] - (pivot[r, c] * pivot[d, c]) * reciprocal[c]
                    else:
                        pivot[r, d] = pivot[r, d] - lower[r] * pivot[d, c]
            for r in range(c + 1, PANEL):
                rows[r] = rows[r] - lower[r] * rows[c]
                for k in range(c):
                    inverse[r, k] = inverse[r, k] - lower[r] * inverse[c, k]
                inverse[r, c] = -lower[r]
        for r in range(PANEL):
            done = jnp.where(lane < start + PANEL, rows[r], 0.0) * lax.rsqrt(pivot[r, r])
            out_ref[start + r : start + r + 1, :] = done[0:1, :]
        if p == panels - 1:
            break
        scaled = [rows[r] * reciprocal[r] for r in range(PANEL)]
        eliminate = []
        for c in range(PANEL):
            total = scaled[c]
            for r in range(c + 1, PANEL):
                total = total + inverse[r, c] * scaled[r]
            eliminate.append(total)
        for i in range(p + 1, panels):
            steps = [full(tiles[i][:, start + c : start + c + 1]) * eliminate[c] for c in range(PANEL)]
            tiles[i] = jnp.where(inside, 0.0, tiles[i]) - add_pairs(steps)


def start_kernel(after_ref, start_ref, out_ref, factor_ref, spread_ref):
    del after_ref
    rows = start_ref[...].T
    inverse_factor(dot_full(rows, rows, NT), factor_ref, spread_ref)
    out_ref[...] = dot_full(factor_ref[...], rows, NN)


def split_kernel(rows_ref, high_ref, low_ref):
    order = rows_ref.shape[1]
    extra = high_ref.shape[1] - order
    for target, values in zip((high_ref, low_ref), split(rows_ref[...])):
        target[:, 0:order] = values
        target[:, order : order + extra] = values[:, :extra]


def gram_kernel(where_ref, own_high, own_low, other_ref, *refs):
    outs, (high_ref, low_ref) = refs[:-2], refs[-2:]
    band = outs[0].shape[1]
    rows, order = other_ref.shape
    extra = high_ref.shape[1] - order
    for own, target, values in zip((own_high, own_low), (high_ref, low_ref), split(other_ref[...])):
        target[0:rows, :] = own[...]
        target[rows : 2 * rows, 0:order] = values
        target[rows : 2 * rows, order : order + extra] = values[:, :extra]
    group, core = where_ref[0], where_ref[1]
    for k, out in enumerate(outs):
        first = pl.multiple_of((2 * jnp.bitwise_xor(group, k) + core) * BLOCK, BLOCK)
        left = [ref[:, pl.ds(first, BLOCK)].astype(jnp.float32).T.astype(jnp.bfloat16) for ref in (high_ref, low_ref)]
        right = [ref[:, pl.ds(first, band)] for ref in (high_ref, low_ref)]
        out[...] = dot_split(left, right, NN)


def cut_kernel(count, where_ref, after_ref, *refs):
    del after_ref
    terms, outs = refs[: len(refs) - count], refs[len(refs) - count :]
    rows = outs[0].shape[0]
    plane = where_ref[2]
    for k, out in enumerate(outs):
        piece = pl.ds(pl.multiple_of(jnp.bitwise_xor(plane, k) * rows, rows), rows)
        total = terms[0][piece, :]
        for term in terms[1:]:
            total = total + term[piece, :]
        out[...] = total


def add_kernel(*refs):
    total = refs[0][...]
    for term in refs[1:-1]:
        total = total + term[...]
    refs[-1][...] = total


def join_kernel(where_ref, *refs):
    pieces, out = refs[:-1], refs[-1]
    rows = pieces[0].shape[0]
    plane = where_ref[2]
    for k, piece in enumerate(pieces):
        out[pl.ds(pl.multiple_of(jnp.bitwise_xor(plane, k) * rows, rows), rows), :] = piece[...]


def sweeps(basis_ref, image_ref, last_ref, high_ref, low_ref, factor_ref, spread_ref):
    def times_gram(rows):
        return dot_split(split(rows), (high_ref[...], low_ref[...]), NN)

    def body(step, carry):
        image = image_ref[...]
        halves = split(image)
        inner = dot_split(halves, halves, NT)
        following = times_gram(image)
        inverse_factor(inner, factor_ref, spread_ref)
        image_ref[...] = dot_split(split(factor_ref[...]), split(following), NN)
        return carry

    image_ref[...] = times_gram(basis_ref[...])
    lax.fori_loop(0, ITERS - 1, body, 0)
    image = image_ref[...]
    last_ref[...] = dot_full(image, image, NT)


def last_kernel(matrix_ref, out_ref, spread_ref):
    inverse_factor(matrix_ref[...], out_ref, spread_ref)


def banded_kernel(blocks, where_ref, basis_ref, *refs):
    bands, rest = refs[:-6], refs[-6:]
    high_ref, low_ref = rest[2:4]
    group, core = where_ref[0], where_ref[1]
    half = len(bands) // 2
    for place, band in enumerate(bands):
        side = core if place < half else 1 - core
        row = 2 * jnp.bitwise_xor(group, place % half) + side
        rows = pl.ds(pl.multiple_of(row * BLOCK, BLOCK), BLOCK)
        for k in range(blocks // 2 + 1):
            column = lax.rem(row + k, blocks)
            columns = pl.ds(pl.multiple_of(column * BLOCK, BLOCK), BLOCK)
            part = band[:, BLOCK * k : BLOCK * (k + 1)]
            high_ref[rows, columns], low_ref[rows, columns] = split(part)
            if 0 < k < blocks // 2:
                high_ref[columns, rows], low_ref[columns, rows] = split(part.T)
    sweeps(basis_ref, *rest)


def whole_kernel(basis_ref, gram_ref, *rest):
    rest[2][...], rest[3][...] = split(gram_ref[...])
    sweeps(basis_ref, *rest)


def tail_kernel(cells_three, where_ref, inner_ref, image_ref, *refs):
    fields, (out_ref, factor_ref, spread_ref, own_ref, all_ref) = refs[:-5], refs[-5:]
    size = fields[0].shape[0]
    cells_two = size // cells_three
    image = split(image_ref[...])
    raw = [dot_split(split(field[...]), image, NT) for field in fields]
    inverse_factor(inner_ref[...], factor_ref, spread_ref)
    factor = factor_ref[...]
    plane = where_ref[2]
    for k, part in enumerate(raw):
        core = dot_full(part, factor, NT)
        if k == 0:
            own_ref[...] = core
        place = pl.multiple_of(jnp.bitwise_xor(plane, k) * size, size)
        all_ref[pl.ds(place, size), :] = core
    own = [own_ref[pl.ds(k, cells_two, stride=cells_three), :] for k in range(cells_three)]
    every = [
        jnp.concatenate(
            [all_ref[pl.ds(size * q + k, cells_two, stride=cells_three), :] for q in range(len(fields))], axis=0
        )
        for k in range(cells_three)
    ]
    out_ref[...] = dot_full(jnp.concatenate(own, axis=1), jnp.concatenate(every, axis=1), NT)


def call(kernel, outs, name, operands, scratch=(), scalars=0, order_only=(), flops=0, dtype=jnp.float32):
    shapes = [jax.ShapeDtypeStruct(shape, dtype) for shape in outs]
    touched = sum(operand.size for operand in operands) + sum(shape.size for shape in shapes)
    result = pl.pallas_call(
        kernel,
        out_shape=shapes,
        in_specs=[SCALARS] * scalars
        + [pl.BlockSpec(memory_space=pl.ANY)] * len(order_only)
        + [VMEM] * (len(operands) - scalars),
        out_specs=[VMEM] * len(shapes),
        scratch_shapes=list(scratch),
        compiler_params=pltpu.CompilerParams(vmem_limit_bytes=32 * 2**20),
        cost_estimate=pl.CostEstimate(flops=flops, bytes_accessed=4 * touched, transcendentals=0),
        name=name,
    )(*operands[:scalars], *order_only, *operands[scalars:])
    return result if len(outs) > 1 else result[0]


def swap(array, axis, mask):
    return lax.ppermute(array, axis, [(i, i ^ mask) for i in range(lax.axis_size(axis))])


def gather_planes(rows, planes):
    mask = planes // 2
    found = {0: rows}
    while mask:
        found.update({k | mask: swap(found[k], "narrow", mask) for k in list(found)})
        mask //= 2
    return [found[k] for k in range(1, planes)]


def shards(field, start_block):
    cells_two, cells_three, order = field.shape
    rank = start_block.shape[1]
    narrow, wide = lax.axis_size("narrow"), lax.axis_size("wide")
    unfolded = field.reshape(cells_two * cells_three, order)
    cells = unfolded.shape[0]
    place, plane = lax.axis_index("wide"), lax.axis_index("narrow")
    where = jnp.stack([place // 2, place % 2, plane]).astype(jnp.int32)
    spread = pltpu.VMEM((2 * PANEL * PANEL, rank), jnp.float32)

    def orthonormal_start(after):
        return call(
            start_kernel,
            [(rank, order)],
            "orth_start",
            [start_block],
            [pltpu.VMEM((rank, rank), jnp.float32), spread],
            order_only=[after],
            flops=10**9,
        )

    scratch = [
        pltpu.VMEM((order, order), jnp.bfloat16),
        pltpu.VMEM((order, order), jnp.bfloat16),
        pltpu.VMEM((rank, rank), jnp.float32),
        spread,
    ]
    results = [(rank, order), (rank, rank)]
    blocks = order // BLOCK
    if wide == blocks and narrow & (narrow - 1) == 0 and BLOCK % (8 * narrow) == 0:
        groups = wide // 2
        band = BLOCK * (blocks // 2 + 1)
        extended = (cells, order + band - BLOCK)
        other = swap(unfolded, "wide", 1)
        fields = [unfolded] + gather_planes(unfolded, narrow)
        own = call(split_kernel, [extended] * 2, "split_field", [unfolded], dtype=jnp.bfloat16)
        parts = call(
            gram_kernel,
            [(BLOCK, band)] * groups,
            "gram_band",
            [where, *own, other],
            [pltpu.VMEM((2 * cells, extended[1]), jnp.bfloat16)] * 2,
            scalars=1,
        )
        arrived = [swap(parts[k], "wide", 2 * k) for k in range(1, groups)]
        basis = orthonormal_start(parts[0])
        cuts = call(
            functools.partial(cut_kernel, narrow),
            [(BLOCK // narrow, band)] * narrow,
            "sum_groups",
            [where, parts[0], *arrived],
            scalars=1,
            order_only=[basis],
        )
        arrived = [swap(cuts[k], "narrow", k) for k in range(1, narrow)]
        piece = call(add_kernel, [(BLOCK // narrow, band)], "sum_planes", [cuts[0], *arrived])
        arrived = [swap(piece, "narrow", k) for k in range(1, narrow)]
        joined = call(join_kernel, [(BLOCK, band)], "join_planes", [where, piece, *arrived], scalars=1)
        bands = [joined] + [swap(joined, "wide", 2 * k) for k in range(1, groups)]
        bands = bands + [swap(part, "wide", 1) for part in bands]
        image, inner = call(
            functools.partial(banded_kernel, blocks),
            results,
            "sweeps",
            [where, basis, *bands],
            scratch,
            scalars=1,
        )
        total = call(
            functools.partial(tail_kernel, cells_three),
            [(cells_two, narrow * cells_two)],
            "core_pairs",
            [where, inner, image, *fields],
            [
                pltpu.VMEM((rank, rank), jnp.float32),
                spread,
                pltpu.VMEM((cells, rank), jnp.float32),
                pltpu.VMEM((narrow * cells, rank), jnp.float32),
            ],
            scalars=1,
        )
        mask = 1
        while mask < wide:
            total = total + swap(total, "wide", mask)
            mask *= 2
        columns = narrow * cells_two // wide
        finished = lax.dynamic_slice_in_dim(total, place * columns, columns, 1)
    else:
        basis = orthonormal_start(start_block)
        gram = lax.dot_general(unfolded, unfolded, (((0,), (0,)), ((), ())), precision=HIGHEST)
        gram = lax.psum(gram, ("narrow", "wide"))
        image, inner = call(whole_kernel, results, "sweeps", [basis, gram], scratch)
        factor = call(last_kernel, [(rank, rank)], "last_factor", [inner], [spread])
        core = lax.dot_general(unfolded, image, NT, precision=HIGHEST)
        core = lax.dot_general(core, factor, NT, precision=HIGHEST)
        merged = core.reshape(cells_two, cells_three * rank)
        everyone = lax.all_gather(merged, "narrow", axis=0, tiled=True)
        part = lax.dot_general(merged, everyone, NT, precision=HIGHEST)
        finished = lax.psum_scatter(part, "wide", scatter_dimension=1, tiled=True)
    return finished / (rank * cells_three * wide)


def solution(mesh):
    return jax.shard_map(
        shards,
        mesh=mesh,
        in_specs=(P("narrow", "wide", None), P()),
        out_specs=P("narrow", "wide"),
        check_vma=False,
    )
```

```python
import functools
import jax
import jax.numpy as jnp
from jax import lax
from jax.experimental import pallas as pl
from jax.experimental.pallas import tpu as pltpu
from jax.sharding import PartitionSpec as P

ITERS = 4
BLOCK = 128
PANEL = 8
HIGHEST = lax.Precision.HIGHEST
NN = (((1,), (0,)), ((), ()))
NT = (((1,), (1,)), ((), ()))
VMEM = pl.BlockSpec(memory_space=pltpu.VMEM)


def split(values):
    high = values.astype(jnp.bfloat16)
    return high, (values - high.astype(jnp.float32)).astype(jnp.bfloat16)


def dot_bf16(left, right, dims):
    return lax.dot_general(left, right, dims, preferred_element_type=jnp.float32)


def dot_split(left, right, dims):
    (left_high, left_low), (right_high, right_low) = left, right
    return (
        dot_bf16(left_high, right_high, dims)
        + (dot_bf16(left_low, right_high, dims) + dot_bf16(left_high, right_low, dims))
    )


def dot_full(left, right, dims):
    return lax.dot_general(left, right, dims, precision=HIGHEST, preferred_element_type=jnp.float32)


def add_pairs(terms):
    terms = list(terms)
    while len(terms) > 1:
        pairs = [terms[i] + terms[i + 1] for i in range(0, len(terms) - 1, 2)]
        terms = pairs + terms[2 * len(pairs) :]
    return terms[0]


def inverse_factor(matrix, out_ref, scratch):
    order = matrix.shape[0]
    panels = order // PANEL
    tiles = [matrix[PANEL * i : PANEL * (i + 1), :] for i in range(panels)]
    lane = lax.broadcasted_iota(jnp.int32, (PANEL, order), 1)

    def full(part):
        return jnp.broadcast_to(part, (PANEL, order))

    for p in range(panels):
        tile, start = tiles[p], PANEL * p
        base = PANEL * PANEL * (p % 2)
        inside = (lane >= start) & (lane < start + PANEL)
        for c in range(PANEL):
            scratch[base + PANEL * c : base + PANEL * (c + 1), :] = full(tile[:, start + c : start + c + 1])
        pivot = {
            (r, c): full(scratch[base + PANEL * c + r : base + PANEL * c + r + 1, :])
            for c in range(PANEL)
            for r in range(c, PANEL)
        }
        rows = [
            jnp.where(inside, jnp.where(lane == start + c, 1.0, 0.0), full(tile[c : c + 1, :]))
            for c in range(PANEL)
        ]
        reciprocal, inverse = {}, {}
        for c in range(PANEL):
            reciprocal[c] = 1.0 / pivot[c, c]
            lower = {r: pivot[r, c] * reciprocal[c] for r in range(c + 1, PANEL)}
            for d in range(c + 1, PANEL):
                for r in range(d, PANEL):
                    if r == c + 1:
                        pivot[r, d] = pivot[r, d] - (pivot[r, c] * pivot[d, c]) * reciprocal[c]
                    else:
                        pivot[r, d] = pivot[r, d] - lower[r] * pivot[d, c]
            for r in range(c + 1, PANEL):
                rows[r] = rows[r] - lower[r] * rows[c]
                for k in range(c):
                    inverse[r, k] = inverse[r, k] - lower[r] * inverse[c, k]
                inverse[r, c] = -lower[r]
        for r in range(PANEL):
            done = jnp.where(lane < start + PANEL, rows[r], 0.0) * lax.rsqrt(pivot[r, r])
            out_ref[start + r : start + r + 1, :] = done[0:1, :]
        if p == panels - 1:
            break
        scaled = [rows[r] * reciprocal[r] for r in range(PANEL)]
        eliminate = []
        for c in range(PANEL):
            total = scaled[c]
            for r in range(c + 1, PANEL):
                total = total + inverse[r, c] * scaled[r]
            eliminate.append(total)
        for i in range(p + 1, panels):
            steps = [full(tiles[i][:, start + c : start + c + 1]) * eliminate[c] for c in range(PANEL)]
            tiles[i] = jnp.where(inside, 0.0, tiles[i]) - add_pairs(steps)


def start_kernel(after_ref, start_ref, out_ref, factor_ref, spread_ref):
    del after_ref
    rows = start_ref[...].T
    inverse_factor(dot_full(rows, rows, NT), factor_ref, spread_ref)
    out_ref[...] = dot_full(factor_ref[...], rows, NN)


def split_kernel(rows_ref, high_ref, low_ref):
    order = rows_ref.shape[1]
    extra = high_ref.shape[1] - order
    for target, values in zip((high_ref, low_ref), split(rows_ref[...])):
        target[:, 0:order] = values
        target[:, order : order + extra] = values[:, :extra]


def chip_and_core():
    place = lax.axis_index("wide")
    return place // 2, lax.rem(place, 2)


def gram_kernel(own_high, own_low, other_ref, *refs):
    outs, (high_ref, low_ref) = refs[:-2], refs[-2:]
    band = outs[0].shape[1]
    rows, order = other_ref.shape
    extra = high_ref.shape[1] - order
    for own, target, values in zip((own_high, own_low), (high_ref, low_ref), split(other_ref[...])):
        target[0:rows, :] = own[...]
        target[rows : 2 * rows, 0:order] = values
        target[rows : 2 * rows, order : order + extra] = values[:, :extra]
    group, core = chip_and_core()
    half = BLOCK // 2
    first_keep, first_send, second_keep, second_send = outs
    upper = [first_keep, first_send, first_keep, first_send]
    lower = [second_keep, second_keep, second_send, second_send]
    for k in range(len(outs)):
        first = pl.multiple_of((2 * jnp.bitwise_xor(group, k) + core) * BLOCK, BLOCK)
        left = [ref[:, pl.ds(first, BLOCK)].astype(jnp.float32).T.astype(jnp.bfloat16) for ref in (high_ref, low_ref)]
        right = [ref[:, pl.ds(first, band)] for ref in (high_ref, low_ref)]
        rows = dot_split(left, right, NN)
        upper[k][half * (k // 2) : half * (k // 2 + 1), :] = rows[:half]
        lower[k][half * (k % 2) : half * (k % 2 + 1), :] = rows[half:]


def halve_kernel(after_ref, kept_first, got_first, kept_second, got_second, *outs):
    del after_ref
    half = kept_first.shape[0] // 2
    for kept, got, (own, send) in ((kept_first, got_first, outs[:2]), (kept_second, got_second, outs[2:])):
        own[...] = kept[:half, :] + got[:half, :]
        send[...] = kept[half:, :] + got[half:, :]


def cut_kernel(first, got_first, second, got_second, *outs):
    rows = outs[0].shape[0] // 2
    plane = lax.axis_index("narrow")
    for k, out in enumerate(outs):
        piece = pl.ds(pl.multiple_of(jnp.bitwise_xor(plane, k) * rows, rows), rows)
        out[:rows, :] = first[piece, :] + got_first[piece, :]
        out[rows:, :] = second[piece, :] + got_second[piece, :]


def add_kernel(*refs):
    total = refs[0][...]
    for term in refs[1:-1]:
        total = total + term[...]
    refs[-1][...] = total


def join_kernel(*refs):
    pieces, (first, second) = refs[:-2], refs[-2:]
    rows = pieces[0].shape[0] // 2
    plane = lax.axis_index("narrow")
    for k, piece in enumerate(pieces):
        place = pl.ds(pl.multiple_of(jnp.bitwise_xor(plane, k) * rows, rows), rows)
        first[place, :] = piece[:rows, :]
        second[place, :] = piece[rows:, :]


def stack_kernel(first, got_first, second, got_second, first_out, second_out):
    half = first.shape[0]
    for own, got, out in ((first, got_first, first_out), (second, got_second, second_out)):
        out[:half, :] = own[...]
        out[half:, :] = got[...]


def sweeps(basis_ref, field_ref, image_ref, inner_ref, raw_ref, high_ref, low_ref, factor_ref, spread_ref, basis_scratch):
    def times_gram(rows):
        return dot_split(split(rows), (high_ref[...], low_ref[...]), NN)

    def body(step, carry):
        image = basis_scratch[...]
        halves = split(image)
        inner = dot_split(halves, halves, NT)
        following = times_gram(image)
        inverse_factor(inner, factor_ref, spread_ref)
        basis_scratch[...] = dot_split(split(factor_ref[...]), split(following), NN)
        return carry

    basis_scratch[...] = times_gram(basis_ref[...])
    lax.fori_loop(0, ITERS - 2, body, 0)
    image = basis_scratch[...]
    following = times_gram(image)
    image_ref[...] = following
    inner_ref[...] = dot_full(image, image, NT)
    raw_ref[...] = dot_full(field_ref[...], following, NT)


def last_kernel(image_ref, inner_ref, out_ref, factor_ref, spread_ref):
    inverse_factor(inner_ref[...], factor_ref, spread_ref)
    before = factor_ref[...]
    image = dot_full(before, image_ref[...], NN)
    inverse_factor(dot_full(image, image, NT), factor_ref, spread_ref)
    out_ref[...] = dot_full(factor_ref[...], before, NN)


def banded_kernel(blocks, basis_ref, field_ref, *refs):
    bands, rest = refs[:-8], refs[-8:]
    high_ref, low_ref = rest[3:5]
    group, core = chip_and_core()
    half = BLOCK // 2
    halves = {0: ((0, 0), (1, 0)), 1: ((2, 0), (1, 1)), 2: ((0, 1), (3, 0)), 3: ((2, 1), (3, 1))}
    for place in range(2 * len(halves)):
        side = core if place < len(halves) else 1 - core
        row = 2 * jnp.bitwise_xor(group, place % len(halves)) + side
        upper, lower = [
            bands[number + 4 * (place // len(halves))].at[half * part : half * (part + 1)]
            for number, part in halves[place % len(halves)]
        ]
        rows = pl.ds(pl.multiple_of(row * BLOCK, BLOCK), BLOCK)
        for k in range(blocks // 2 + 1):
            column = lax.rem(row + k, blocks)
            columns = pl.ds(pl.multiple_of(column * BLOCK, BLOCK), BLOCK)
            inside = slice(BLOCK * k, BLOCK * (k + 1))
            part = jnp.concatenate([upper[:, inside], lower[:, inside]], axis=0)
            high_ref[rows, columns], low_ref[rows, columns] = split(part)
            if 0 < k < blocks // 2:
                high_ref[columns, rows], low_ref[columns, rows] = split(part.T)
    sweeps(basis_ref, field_ref, *rest)


def whole_kernel(basis_ref, field_ref, gram_ref, *rest):
    rest[3][...], rest[4][...] = split(gram_ref[...])
    sweeps(basis_ref, field_ref, *rest)


def tail_kernel(cells_three, factor_ref, *refs):
    raw, (out_ref, own_ref, all_ref) = refs[:-3], refs[-3:]
    size = raw[0].shape[0]
    cells_two = size // cells_three
    planes = len(raw)
    factor = factor_ref[...]
    plane = lax.axis_index("narrow")
    for k, part in enumerate(raw):
        core = dot_full(part[...], factor, NT)
        if k == 0:
            own_ref[...] = core
        place = pl.multiple_of(jnp.bitwise_xor(plane, k) * size, size)
        all_ref[pl.ds(place, size), :] = core
    own = [own_ref[pl.ds(k, cells_two, stride=cells_three), :] for k in range(cells_three)]
    every = [
        jnp.concatenate(
            [all_ref[pl.ds(size * q + k, cells_two, stride=cells_three), :] for q in range(planes)], axis=0
        )
        for k in range(cells_three)
    ]
    out_ref[...] = dot_full(jnp.concatenate(own, axis=1), jnp.concatenate(every, axis=1), NT)


def call(kernel, outs, name, operands, scratch=(), order_only=(), flops=0, dtype=jnp.float32):
    shapes = [jax.ShapeDtypeStruct(shape, dtype) for shape in outs]
    touched = sum(operand.size for operand in operands) + sum(shape.size for shape in shapes)
    result = pl.pallas_call(
        kernel,
        out_shape=shapes,
        in_specs=[pl.BlockSpec(memory_space=pl.ANY)] * len(order_only) + [VMEM] * len(operands),
        out_specs=[VMEM] * len(shapes),
        scratch_shapes=list(scratch),
        compiler_params=pltpu.CompilerParams(vmem_limit_bytes=32 * 2**20),
        cost_estimate=pl.CostEstimate(flops=flops, bytes_accessed=4 * touched, transcendentals=0),
        name=name,
    )(*order_only, *operands)
    return result if len(outs) > 1 else result[0]


def swap(array, axis, mask):
    return lax.ppermute(array, axis, [(i, i ^ mask) for i in range(lax.axis_size(axis))])


def shards(field, start_block):
    cells_two, cells_three, order = field.shape
    rank = start_block.shape[1]
    narrow, wide = lax.axis_size("narrow"), lax.axis_size("wide")
    unfolded = field.reshape(cells_two * cells_three, order)
    cells = unfolded.shape[0]
    place = lax.axis_index("wide")
    spread = pltpu.VMEM((2 * PANEL * PANEL, rank), jnp.float32)

    def orthonormal_start(after):
        return call(
            start_kernel,
            [(rank, order)],
            "orth_start",
            [start_block],
            [pltpu.VMEM((rank, rank), jnp.float32), spread],
            order_only=[after],
            flops=10**9,
        )

    def last_factors(image, inner):
        return call(
            last_kernel,
            [(rank, rank)],
            "last_factors",
            [image, inner],
            [pltpu.VMEM((rank, rank), jnp.float32), spread],
            flops=10**9,
        )

    scratch = [
        pltpu.VMEM((order, order), jnp.bfloat16),
        pltpu.VMEM((order, order), jnp.bfloat16),
        pltpu.VMEM((rank, rank), jnp.float32),
        spread,
        pltpu.VMEM((rank, order), jnp.float32),
    ]
    results = [(rank, order), (rank, rank), (cells, rank)]
    blocks = order // BLOCK
    if wide == blocks and narrow & (narrow - 1) == 0 and BLOCK % (8 * narrow) == 0:
        groups = wide // 2
        band = BLOCK * (blocks // 2 + 1)
        extended = (cells, order + band - BLOCK)
        other = swap(unfolded, "wide", 1)
        own = call(split_kernel, [extended] * 2, "split_field", [unfolded], dtype=jnp.bfloat16)
        first_kept, first_sent, second_kept, second_sent = call(
            gram_kernel,
            [(BLOCK, band)] * groups,
            "gram_band",
            [*own, other],
            [pltpu.VMEM((2 * cells, extended[1]), jnp.bfloat16)] * 2,
            flops=10**9,
        )
        first_got, second_got = swap(first_sent, "wide", 2), swap(second_sent, "wide", 4)
        basis = orthonormal_start(first_kept)
        first, first_sent, second, second_sent = call(
            halve_kernel,
            [(BLOCK // 2, band)] * 4,
            "sum_pairs",
            [first_kept, first_got, second_kept, second_got],
            order_only=[basis],
        )
        cuts = call(
            cut_kernel,
            [(BLOCK // narrow, band)] * narrow,
            "sum_groups",
            [first, swap(first_sent, "wide", 4), second, swap(second_sent, "wide", 2)],
        )
        arrived = [swap(cuts[k], "narrow", k) for k in range(1, narrow)]
        piece = call(add_kernel, [(BLOCK // narrow, band)], "sum_planes", [cuts[0], *arrived])
        arrived = [swap(piece, "narrow", k) for k in range(1, narrow)]
        first, second = call(
            join_kernel,
            [(BLOCK // 2, band)] * 2,
            "join_planes",
            [piece, *arrived],
        )
        stacks = call(
            stack_kernel,
            [(BLOCK, band)] * 2,
            "stack_pairs",
            [first, swap(first, "wide", 4), second, swap(second, "wide", 2)],
        )
        stacks = [*stacks, swap(stacks[0], "wide", 2), swap(stacks[1], "wide", 4)]
        bands = stacks + [swap(stack, "wide", 1) for stack in stacks]
        image, inner, raw = call(
            functools.partial(banded_kernel, blocks),
            results,
            "sweeps",
            [basis, unfolded, *bands],
            scratch,
        )
        raws = [raw] + [swap(raw, "narrow", k) for k in range(1, narrow)]
        factor = last_factors(image, inner)
        total = call(
            functools.partial(tail_kernel, cells_three),
            [(cells_two, narrow * cells_two)],
            "core_pairs",
            [factor, *raws],
            [pltpu.VMEM((cells, rank), jnp.float32), pltpu.VMEM((narrow * cells, rank), jnp.float32)],
        )
        total = add_pairs([total] + [swap(total, "wide", k) for k in range(1, 4)])
        total = total + swap(total, "wide", 4)
        columns = narrow * cells_two // wide
        finished = lax.dynamic_slice_in_dim(total, place * columns, columns, 1)
    else:
        basis = orthonormal_start(start_block)
        gram = lax.dot_general(unfolded, unfolded, (((0,), (0,)), ((), ())), precision=HIGHEST)
        gram = lax.psum(gram, ("narrow", "wide"))
        image, inner, raw = call(whole_kernel, results, "sweeps", [basis, unfolded, gram], scratch)
        core = lax.dot_general(raw, last_factors(image, inner), NT, precision=HIGHEST)
        merged = core.reshape(cells_two, cells_three * rank)
        everyone = lax.all_gather(merged, "narrow", axis=0, tiled=True)
        part = lax.dot_general(merged, everyone, NT, precision=HIGHEST)
        finished = lax.psum_scatter(part, "wide", scatter_dimension=1, tiled=True)
    return finished / (rank * cells_three * wide)


def solution(mesh):
    return jax.shard_map(
        shards,
        mesh=mesh,
        in_specs=(P("narrow", "wide", None), P()),
        out_specs=P("narrow", "wide"),
        check_vma=False,
    )
```

```python
import functools
import jax
import jax.numpy as jnp
from jax import lax
from jax.experimental import pallas as pl
from jax.experimental.pallas import tpu as pltpu
from jax.sharding import PartitionSpec as P

ITERS = 4
BLOCK = 128
PANEL = 8
HIGHEST = lax.Precision.HIGHEST
NN = (((1,), (0,)), ((), ()))
NT = (((1,), (1,)), ((), ()))
VMEM = pl.BlockSpec(memory_space=pltpu.VMEM)


def split(values):
    high = values.astype(jnp.bfloat16)
    return high, (values - high.astype(jnp.float32)).astype(jnp.bfloat16)


def dot_bf16(left, right, dims):
    return lax.dot_general(left, right, dims, preferred_element_type=jnp.float32)


def dot_split(left, right, dims):
    (left_high, left_low), (right_high, right_low) = left, right
    return (
        dot_bf16(left_high, right_high, dims)
        + (dot_bf16(left_low, right_high, dims) + dot_bf16(left_high, right_low, dims))
    )


def dot_full(left, right, dims):
    return lax.dot_general(left, right, dims, precision=HIGHEST, preferred_element_type=jnp.float32)


def add_pairs(terms):
    terms = list(terms)
    while len(terms) > 1:
        pairs = [terms[i] + terms[i + 1] for i in range(0, len(terms) - 1, 2)]
        terms = pairs + terms[2 * len(pairs) :]
    return terms[0]


def inverse_factor(matrix, out_ref, scratch):
    order = matrix.shape[0]
    panels = order // PANEL
    tiles = [matrix[PANEL * i : PANEL * (i + 1), :] for i in range(panels)]
    lane = lax.broadcasted_iota(jnp.int32, (PANEL, order), 1)

    def full(part):
        return jnp.broadcast_to(part, (PANEL, order))

    for p in range(panels):
        tile, start = tiles[p], PANEL * p
        base = PANEL * PANEL * (p % 2)
        inside = (lane >= start) & (lane < start + PANEL)
        for c in range(PANEL):
            scratch[base + PANEL * c : base + PANEL * (c + 1), :] = full(tile[:, start + c : start + c + 1])
        pivot = {
            (r, c): full(scratch[base + PANEL * c + r : base + PANEL * c + r + 1, :])
            for c in range(PANEL)
            for r in range(c, PANEL)
        }
        rows = [
            jnp.where(inside, jnp.where(lane == start + c, 1.0, 0.0), full(tile[c : c + 1, :]))
            for c in range(PANEL)
        ]
        reciprocal, inverse = {}, {}
        for c in range(PANEL):
            reciprocal[c] = 1.0 / pivot[c, c]
            lower = {r: pivot[r, c] * reciprocal[c] for r in range(c + 1, PANEL)}
            for d in range(c + 1, PANEL):
                for r in range(d, PANEL):
                    if r == c + 1:
                        pivot[r, d] = pivot[r, d] - (pivot[r, c] * pivot[d, c]) * reciprocal[c]
                    else:
                        pivot[r, d] = pivot[r, d] - lower[r] * pivot[d, c]
            for r in range(c + 1, PANEL):
                rows[r] = rows[r] - lower[r] * rows[c]
                for k in range(c):
                    inverse[r, k] = inverse[r, k] - lower[r] * inverse[c, k]
                inverse[r, c] = -lower[r]
        for r in range(PANEL):
            done = jnp.where(lane < start + PANEL, rows[r], 0.0) * lax.rsqrt(pivot[r, r])
            out_ref[start + r : start + r + 1, :] = done[0:1, :]
        if p == panels - 1:
            break
        scaled = [rows[r] * reciprocal[r] for r in range(PANEL)]
        eliminate = []
        for c in range(PANEL):
            total = scaled[c]
            for r in range(c + 1, PANEL):
                total = total + inverse[r, c] * scaled[r]
            eliminate.append(total)
        for i in range(p + 1, panels):
            steps = [full(tiles[i][:, start + c : start + c + 1]) * eliminate[c] for c in range(PANEL)]
            tiles[i] = jnp.where(inside, 0.0, tiles[i]) - add_pairs(steps)


def start_kernel(after_ref, start_ref, out_ref, factor_ref, spread_ref):
    del after_ref
    rows = start_ref[...].T
    inverse_factor(dot_full(rows, rows, NT), factor_ref, spread_ref)
    out_ref[...] = dot_full(factor_ref[...], rows, NN)


def split_kernel(rows_ref, high_ref, low_ref):
    order = rows_ref.shape[1]
    extra = high_ref.shape[1] - order
    for target, values in zip((high_ref, low_ref), split(rows_ref[...])):
        target[:, 0:order] = values
        target[:, order : order + extra] = values[:, :extra]


def chip_and_core():
    place = lax.axis_index("wide")
    return place // 2, lax.rem(place, 2)


def gram_kernel(own_high, own_low, other_ref, *refs):
    outs, (high_ref, low_ref, corner_ref) = refs[:-3], refs[-3:]
    half, band = outs[0].shape[0] // 2, outs[0].shape[1]
    rows, order = other_ref.shape
    extra = high_ref.shape[1] - order
    for own, target, values in zip((own_high, own_low), (high_ref, low_ref), split(other_ref[...])):
        target[0:rows, :] = own[...]
        target[rows : 2 * rows, 0:order] = values
        target[rows : 2 * rows, order : order + extra] = values[:, :extra]
    group, core = chip_and_core()
    first_keep, first_send, second_keep, second_send = outs
    upper = [first_keep, first_send, first_keep, first_send]
    lower = [second_keep, second_keep, second_send, second_send]
    opposite = order // 2 // BLOCK

    def product(left_block, right_block, width):
        first = pl.multiple_of(left_block * BLOCK, BLOCK)
        second = pl.multiple_of(right_block * BLOCK, BLOCK)
        left = [ref[:, pl.ds(first, BLOCK)].astype(jnp.float32).T.astype(jnp.bfloat16) for ref in (high_ref, low_ref)]
        return dot_split(left, [ref[:, pl.ds(second, width)] for ref in (high_ref, low_ref)], NN)

    for k in range(len(outs)):
        block = 2 * jnp.bitwise_xor(group, k) + core
        corner = lax.rem(block, opposite)
        corner_ref[...] = product(corner, corner + opposite, BLOCK)
        part = corner_ref[pl.ds(pl.multiple_of(block // opposite * (BLOCK // 2), BLOCK // 2), BLOCK // 2), :]
        pieces = BLOCK * BLOCK // 2 // band
        part = jnp.concatenate([part[pieces * i : pieces * (i + 1), :] for i in range(band // BLOCK)], axis=1)
        whole = jnp.concatenate([product(block, block, band), part], axis=0)
        upper[k][half * (k // 2) : half * (k // 2 + 1), :] = whole[:half]
        lower[k][half * (k % 2) : half * (k % 2 + 1), :] = whole[half:]


def halve_kernel(after_ref, kept_first, got_first, kept_second, got_second, *outs):
    del after_ref
    half = kept_first.shape[0] // 2
    for kept, got, (own, send) in ((kept_first, got_first, outs[:2]), (kept_second, got_second, outs[2:])):
        own[...] = kept[:half, :] + got[:half, :]
        send[...] = kept[half:, :] + got[half:, :]


def cut_kernel(first, got_first, second, got_second, *outs):
    rows, columns = first.shape[0], outs[0].shape[1]
    plane = lax.axis_index("narrow")
    for k, out in enumerate(outs):
        piece = pl.ds(pl.multiple_of(jnp.bitwise_xor(plane, k) * columns, columns), columns)
        out[:rows, :] = first[:, piece] + got_first[:, piece]
        out[rows:, :] = second[:, piece] + got_second[:, piece]


def add_kernel(*refs):
    total = refs[0][...]
    for term in refs[1:-1]:
        total = total + term[...]
    refs[-1][...] = total


def join_kernel(*refs):
    pieces, (first, second) = refs[:-2], refs[-2:]
    rows, columns = first.shape[0], pieces[0].shape[1]
    plane = lax.axis_index("narrow")
    for k, piece in enumerate(pieces):
        place = pl.ds(pl.multiple_of(jnp.bitwise_xor(plane, k) * columns, columns), columns)
        first[:, place] = piece[:rows, :]
        second[:, place] = piece[rows:, :]


def stack_kernel(first, got_first, second, got_second, first_out, second_out):
    half = first.shape[0]
    for own, got, out in ((first, got_first, first_out), (second, got_second, second_out)):
        out[:half, :] = own[...]
        out[half:, :] = got[...]


def sweeps(basis_ref, field_ref, image_ref, factor_ref, raw_ref, high_ref, low_ref, spread_ref, basis_scratch):
    def times_gram(rows):
        return dot_split(split(rows), (high_ref[...], low_ref[...]), NN)

    def step(image):
        halves = split(image)
        inner = dot_split(halves, halves, NT)
        following = times_gram(image)
        inverse_factor(inner, factor_ref, spread_ref)
        return following

    def body(number, carry):
        following = step(basis_scratch[...])
        basis_scratch[...] = dot_split(split(factor_ref[...]), split(following), NN)
        return carry

    basis_scratch[...] = times_gram(basis_ref[...])
    lax.fori_loop(0, ITERS - 2, body, 0)
    image = basis_scratch[...]
    inner = dot_full(image, image, NT)
    following = times_gram(image)
    image_ref[...] = following
    raw_ref[...] = dot_full(field_ref[...], following, NT)
    inverse_factor(inner, factor_ref, spread_ref)


def last_kernel(image_ref, before_ref, out_ref, factor_ref, spread_ref):
    before = before_ref[...]
    image = dot_full(before, image_ref[...], NN)
    inverse_factor(dot_full(image, image, NT), factor_ref, spread_ref)
    out_ref[...] = dot_full(factor_ref[...], before, NN)


def banded_kernel(blocks, basis_ref, field_ref, *refs):
    bands, rest = refs[:-7], refs[-7:]
    high_ref, low_ref = rest[3:5]
    group, core = chip_and_core()
    opposite = blocks // 2

    def store(row, column, part, mirror):
        rows = pl.ds(pl.multiple_of(row * BLOCK, BLOCK), BLOCK)
        columns = pl.ds(pl.multiple_of(column * BLOCK, BLOCK), BLOCK)
        high_ref[rows, columns], low_ref[rows, columns] = split(part)
        if mirror:
            high_ref[columns, rows], low_ref[columns, rows] = split(part.T)

    halves = {0: ((0, 0), (1, 0)), 1: ((2, 0), (1, 1)), 2: ((0, 1), (3, 0)), 3: ((2, 1), (3, 1))}
    half, band = bands[0].shape[0] // 2, bands[0].shape[1]
    for stacks, side in ((bands[:4], core), (bands[4:], 1 - core)):
        corners = {}
        for mask, places in halves.items():
            upper, lower = [stacks[number].at[half * part : half * (part + 1)] for number, part in places]
            row = 2 * jnp.bitwise_xor(group, mask) + side
            for k in range(opposite):
                inside = slice(BLOCK * k, BLOCK * (k + 1))
                part = jnp.concatenate([upper[:, inside], lower[: BLOCK - half, inside]], axis=0)
                store(row, lax.rem(row + k, blocks), part, k > 0)
            corners[mask] = jnp.concatenate(
                [lower[BLOCK - half :, BLOCK * i : BLOCK * (i + 1)] for i in range(band // BLOCK)], axis=0
            )
        for mask in (0, 1):
            row = 2 * jnp.bitwise_xor(group, mask) + side
            here, across = corners[mask], corners[mask ^ 2]
            near = row < opposite
            part = jnp.concatenate([jnp.where(near, here, across), jnp.where(near, across, here)], axis=0)
            row = lax.rem(row, opposite)
            store(row, row + opposite, part, True)
    sweeps(basis_ref, field_ref, *rest)


def whole_kernel(basis_ref, field_ref, gram_ref, *rest):
    rest[3][...], rest[4][...] = split(gram_ref[...])
    sweeps(basis_ref, field_ref, *rest)


def tail_kernel(cells_three, factor_ref, *refs):
    raw, (out_ref, own_ref, all_ref) = refs[:-3], refs[-3:]
    size = raw[0].shape[0]
    cells_two = size // cells_three
    planes = len(raw)
    factor = factor_ref[...]
    plane = lax.axis_index("narrow")
    for k, part in enumerate(raw):
        core = dot_full(part[...], factor, NT)
        if k == 0:
            own_ref[...] = core
        place = pl.multiple_of(jnp.bitwise_xor(plane, k) * size, size)
        all_ref[pl.ds(place, size), :] = core
    own = [own_ref[pl.ds(k, cells_two, stride=cells_three), :] for k in range(cells_three)]
    every = [
        jnp.concatenate(
            [all_ref[pl.ds(size * q + k, cells_two, stride=cells_three), :] for q in range(planes)], axis=0
        )
        for k in range(cells_three)
    ]
    out_ref[...] = dot_full(jnp.concatenate(own, axis=1), jnp.concatenate(every, axis=1), NT)


def call(kernel, outs, name, operands, scratch=(), order_only=(), flops=0, dtype=jnp.float32):
    shapes = [jax.ShapeDtypeStruct(shape, dtype) for shape in outs]
    touched = sum(operand.size for operand in operands) + sum(shape.size for shape in shapes)
    result = pl.pallas_call(
        kernel,
        out_shape=shapes,
        in_specs=[pl.BlockSpec(memory_space=pl.ANY)] * len(order_only) + [VMEM] * len(operands),
        out_specs=[VMEM] * len(shapes),
        scratch_shapes=list(scratch),
        compiler_params=pltpu.CompilerParams(vmem_limit_bytes=32 * 2**20),
        cost_estimate=pl.CostEstimate(flops=flops, bytes_accessed=4 * touched, transcendentals=0),
        name=name,
    )(*order_only, *operands)
    return result if len(outs) > 1 else result[0]


def swap(array, axis, mask):
    return lax.ppermute(array, axis, [(i, i ^ mask) for i in range(lax.axis_size(axis))])


def shards(field, start_block):
    cells_two, cells_three, order = field.shape
    rank = start_block.shape[1]
    narrow, wide = lax.axis_size("narrow"), lax.axis_size("wide")
    unfolded = field.reshape(cells_two * cells_three, order)
    cells = unfolded.shape[0]
    place = lax.axis_index("wide")
    spread = pltpu.VMEM((2 * PANEL * PANEL, rank), jnp.float32)

    def orthonormal_start(after):
        return call(
            start_kernel,
            [(rank, order)],
            "orth_start",
            [start_block],
            [pltpu.VMEM((rank, rank), jnp.float32), spread],
            order_only=[after],
            flops=10**9,
        )

    def last_factors(image, before):
        return call(
            last_kernel,
            [(rank, rank)],
            "last_factors",
            [image, before],
            [pltpu.VMEM((rank, rank), jnp.float32), spread],
            flops=10**9,
        )

    scratch = [
        pltpu.VMEM((order, order), jnp.bfloat16),
        pltpu.VMEM((order, order), jnp.bfloat16),
        spread,
        pltpu.VMEM((rank, order), jnp.float32),
    ]
    results = [(rank, order), (rank, rank), (cells, rank)]
    blocks = order // BLOCK
    if wide == blocks and narrow & (narrow - 1) == 0 and blocks // 2 % narrow == 0:
        groups = wide // 2
        band = order // 2
        half = (BLOCK + BLOCK // blocks) // 2
        extended = (cells, order + band - BLOCK)
        other = swap(unfolded, "wide", 1)
        own = call(split_kernel, [extended] * 2, "split_field", [unfolded], dtype=jnp.bfloat16)
        first_kept, first_sent, second_kept, second_sent = call(
            gram_kernel,
            [(2 * half, band)] * groups,
            "gram_band",
            [*own, other],
            [pltpu.VMEM((2 * cells, extended[1]), jnp.bfloat16)] * 2 + [pltpu.VMEM((BLOCK, BLOCK), jnp.float32)],
            flops=10**9,
        )
        first_got, second_got = swap(first_sent, "wide", 2), swap(second_sent, "wide", 4)
        basis = orthonormal_start(first_kept)
        first, first_sent, second, second_sent = call(
            halve_kernel,
            [(half, band)] * 4,
            "sum_pairs",
            [first_kept, first_got, second_kept, second_got],
            order_only=[basis],
        )
        cuts = call(
            cut_kernel,
            [(2 * half, band // narrow)] * narrow,
            "sum_groups",
            [first, swap(first_sent, "wide", 4), second, swap(second_sent, "wide", 2)],
        )
        arrived = [swap(cuts[k], "narrow", k) for k in range(1, narrow)]
        piece = call(add_kernel, [(2 * half, band // narrow)], "sum_planes", [cuts[0], *arrived])
        arrived = [swap(piece, "narrow", k) for k in range(1, narrow)]
        first, second = call(
            join_kernel,
            [(half, band)] * 2,
            "join_planes",
            [piece, *arrived],
        )
        stacks = call(
            stack_kernel,
            [(2 * half, band)] * 2,
            "stack_pairs",
            [first, swap(first, "wide", 4), second, swap(second, "wide", 2)],
        )
        stacks = [*stacks, swap(stacks[0], "wide", 2), swap(stacks[1], "wide", 4)]
        bands = stacks + [swap(stack, "wide", 1) for stack in stacks]
        image, before, raw = call(
            functools.partial(banded_kernel, blocks),
            results,
            "sweeps",
            [basis, unfolded, *bands],
            scratch,
        )
        raws = [raw] + [swap(raw, "narrow", k) for k in range(1, narrow)]
        factor = last_factors(image, before)
        total = call(
            functools.partial(tail_kernel, cells_three),
            [(cells_two, narrow * cells_two)],
            "core_pairs",
            [factor, *raws],
            [pltpu.VMEM((cells, rank), jnp.float32), pltpu.VMEM((narrow * cells, rank), jnp.float32)],
        )
        total = add_pairs([total] + [swap(total, "wide", k) for k in range(1, 4)])
        total = total + swap(total, "wide", 4)
        columns = narrow * cells_two // wide
        finished = lax.dynamic_slice_in_dim(total, place * columns, columns, 1)
    else:
        basis = orthonormal_start(start_block)
        gram = lax.dot_general(unfolded, unfolded, (((0,), (0,)), ((), ())), precision=HIGHEST)
        gram = lax.psum(gram, ("narrow", "wide"))
        image, before, raw = call(whole_kernel, results, "sweeps", [basis, unfolded, gram], scratch)
        core = lax.dot_general(raw, last_factors(image, before), NT, precision=HIGHEST)
        merged = core.reshape(cells_two, cells_three * rank)
        everyone = lax.all_gather(merged, "narrow", axis=0, tiled=True)
        part = lax.dot_general(merged, everyone, NT, precision=HIGHEST)
        finished = lax.psum_scatter(part, "wide", scatter_dimension=1, tiled=True)
    return finished / (rank * cells_three * wide)


def solution(mesh):
    return jax.shard_map(
        shards,
        mesh=mesh,
        in_specs=(P("narrow", "wide", None), P()),
        out_specs=P("narrow", "wide"),
        check_vma=False,
    )
```

```python
import functools
import jax
import jax.numpy as jnp
from jax import lax
from jax.experimental import pallas as pl
from jax.experimental.pallas import tpu as pltpu
from jax.sharding import PartitionSpec as P

ITERS = 4
BLOCK = 128
PANEL = 8
HIGHEST = lax.Precision.HIGHEST
NN = (((1,), (0,)), ((), ()))
NT = (((1,), (1,)), ((), ()))
VMEM = pl.BlockSpec(memory_space=pltpu.VMEM)


def split(values):
    high = values.astype(jnp.bfloat16)
    return high, (values - high.astype(jnp.float32)).astype(jnp.bfloat16)


def dot_bf16(left, right, dims):
    return lax.dot_general(left, right, dims, preferred_element_type=jnp.float32)


def dot_split(left, right, dims):
    (left_high, left_low), (right_high, right_low) = left, right
    return (
        dot_bf16(left_high, right_high, dims)
        + (dot_bf16(left_low, right_high, dims) + dot_bf16(left_high, right_low, dims))
    )


def dot_full(left, right, dims):
    return lax.dot_general(left, right, dims, precision=HIGHEST, preferred_element_type=jnp.float32)


def add_pairs(terms):
    terms = list(terms)
    while len(terms) > 1:
        pairs = [terms[i] + terms[i + 1] for i in range(0, len(terms) - 1, 2)]
        terms = pairs + terms[2 * len(pairs) :]
    return terms[0]


def inverse_factor(matrix, out_ref, scratch):
    order = matrix.shape[0]
    panels = order // PANEL
    tiles = [matrix[PANEL * i : PANEL * (i + 1), :] for i in range(panels)]
    lane = lax.broadcasted_iota(jnp.int32, (PANEL, order), 1)

    def full(part):
        return jnp.broadcast_to(part, (PANEL, order))

    for p in range(panels):
        tile, start = tiles[p], PANEL * p
        base = PANEL * PANEL * (p % 2)
        inside = (lane >= start) & (lane < start + PANEL)
        for c in range(PANEL):
            scratch[base + PANEL * c : base + PANEL * (c + 1), :] = full(tile[:, start + c : start + c + 1])
        pivot = {
            (r, c): full(scratch[base + PANEL * c + r : base + PANEL * c + r + 1, :])
            for c in range(PANEL)
            for r in range(c, PANEL)
        }
        rows = [
            jnp.where(inside, jnp.where(lane == start + c, 1.0, 0.0), full(tile[c : c + 1, :]))
            for c in range(PANEL)
        ]
        reciprocal, inverse = {}, {}
        for c in range(PANEL):
            reciprocal[c] = 1.0 / pivot[c, c]
            lower = {r: pivot[r, c] * reciprocal[c] for r in range(c + 1, PANEL)}
            for d in range(c + 1, PANEL):
                for r in range(d, PANEL):
                    if r == c + 1:
                        pivot[r, d] = pivot[r, d] - (pivot[r, c] * pivot[d, c]) * reciprocal[c]
                    else:
                        pivot[r, d] = pivot[r, d] - lower[r] * pivot[d, c]
            for r in range(c + 1, PANEL):
                rows[r] = rows[r] - lower[r] * rows[c]
                for k in range(c):
                    inverse[r, k] = inverse[r, k] - lower[r] * inverse[c, k]
                inverse[r, c] = -lower[r]
        for r in range(PANEL):
            done = jnp.where(lane < start + PANEL, rows[r], 0.0) * lax.rsqrt(pivot[r, r])
            out_ref[start + r : start + r + 1, :] = done[0:1, :]
        if p == panels - 1:
            break
        scaled = [rows[r] * reciprocal[r] for r in range(PANEL)]
        eliminate = []
        for c in range(PANEL):
            total = scaled[c]
            for r in range(c + 1, PANEL):
                total = total + inverse[r, c] * scaled[r]
            eliminate.append(total)
        for i in range(p + 1, panels):
            steps = [full(tiles[i][:, start + c : start + c + 1]) * eliminate[c] for c in range(PANEL)]
            tiles[i] = jnp.where(inside, 0.0, tiles[i]) - add_pairs(steps)


def start_kernel(after_ref, start_ref, out_ref, factor_ref, spread_ref):
    del after_ref
    rows = start_ref[...].T
    inverse_factor(dot_full(rows, rows, NT), factor_ref, spread_ref)
    out_ref[...] = dot_full(factor_ref[...], rows, NN)


def split_kernel(rows_ref, high_ref, low_ref):
    order = rows_ref.shape[1]
    extra = high_ref.shape[1] - order
    for target, values in zip((high_ref, low_ref), split(rows_ref[...])):
        target[:, 0:order] = values
        target[:, order : order + extra] = values[:, :extra]


def chip_and_core():
    place = lax.axis_index("wide")
    return place // 2, lax.rem(place, 2)


def gram_kernel(own_high, own_low, other_ref, *refs):
    outs, (high_ref, low_ref, corner_ref) = refs[:-3], refs[-3:]
    half, band = outs[0].shape[0] // 2, outs[0].shape[1]
    rows, order = other_ref.shape
    extra = high_ref.shape[1] - order
    for own, target, values in zip((own_high, own_low), (high_ref, low_ref), split(other_ref[...])):
        target[0:rows, :] = own[...]
        target[rows : 2 * rows, 0:order] = values
        target[rows : 2 * rows, order : order + extra] = values[:, :extra]
    group, core = chip_and_core()
    first_keep, first_send, second_keep, second_send = outs
    upper = [first_keep, first_send, first_keep, first_send]
    lower = [second_keep, second_keep, second_send, second_send]
    opposite = order // 2 // BLOCK

    def product(left_block, right_block, width):
        first = pl.multiple_of(left_block * BLOCK, BLOCK)
        second = pl.multiple_of(right_block * BLOCK, BLOCK)
        left = [ref[:, pl.ds(first, BLOCK)].astype(jnp.float32).T.astype(jnp.bfloat16) for ref in (high_ref, low_ref)]
        return dot_split(left, [ref[:, pl.ds(second, width)] for ref in (high_ref, low_ref)], NN)

    for k in range(len(outs)):
        block = 2 * jnp.bitwise_xor(group, k) + core
        corner = lax.rem(block, opposite)
        corner_ref[...] = product(corner, corner + opposite, BLOCK)
        part = corner_ref[pl.ds(pl.multiple_of(block // opposite * (BLOCK // 2), BLOCK // 2), BLOCK // 2), :]
        pieces = BLOCK * BLOCK // 2 // band
        part = jnp.concatenate([part[pieces * i : pieces * (i + 1), :] for i in range(band // BLOCK)], axis=1)
        whole = jnp.concatenate([product(block, block, band), part], axis=0)
        upper[k][half * (k // 2) : half * (k // 2 + 1), :] = whole[:half]
        lower[k][half * (k % 2) : half * (k % 2 + 1), :] = whole[half:]


def halve_kernel(after_ref, cells_ref, kept_first, got_first, kept_second, got_second, *outs):
    del after_ref, cells_ref
    half = kept_first.shape[0] // 2
    for kept, got, (own, send) in ((kept_first, got_first, outs[:2]), (kept_second, got_second, outs[2:])):
        own[...] = kept[:half, :] + got[:half, :]
        send[...] = kept[half:, :] + got[half:, :]


def cut_kernel(first, got_first, second, got_second, *outs):
    rows, columns = first.shape[0], outs[0].shape[1]
    plane = lax.axis_index("narrow")
    for k, out in enumerate(outs):
        piece = pl.ds(pl.multiple_of(jnp.bitwise_xor(plane, k) * columns, columns), columns)
        out[:rows, :] = first[:, piece] + got_first[:, piece]
        out[rows:, :] = second[:, piece] + got_second[:, piece]


def add_kernel(*refs):
    total = refs[0][...]
    for term in refs[1:-1]:
        total = total + term[...]
    refs[-1][...] = total


def join_kernel(*refs):
    pieces, (first, second) = refs[:-2], refs[-2:]
    rows, columns = first.shape[0], pieces[0].shape[1]
    plane = lax.axis_index("narrow")
    for k, piece in enumerate(pieces):
        place = pl.ds(pl.multiple_of(jnp.bitwise_xor(plane, k) * columns, columns), columns)
        first[:, place] = piece[:rows, :]
        second[:, place] = piece[rows:, :]


def stack_kernel(first, got_first, second, got_second, first_out, second_out):
    half = first.shape[0]
    for own, got, out in ((first, got_first, first_out), (second, got_second, second_out)):
        out[:half, :] = own[...]
        out[half:, :] = got[...]


def sweeps(basis_ref, field_ref, image_ref, factor_ref, raw_ref, high_ref, low_ref, spread_ref):
    def times_gram(rows):
        return dot_split(split(rows), (high_ref[...], low_ref[...]), NN)

    image = times_gram(basis_ref[...])
    for number in range(ITERS - 1):
        halves = split(image)
        inner = dot_split(halves, halves, NT)
        following = times_gram(image)
        if number == ITERS - 2:
            image_ref[...] = following
            raw_ref[...] = dot_full(field_ref[...], following, NT)
        inverse_factor(inner, factor_ref, spread_ref)
        image = dot_split(split(factor_ref[...]), split(following), NN)


def halves_kernel(own_field, other_field, sent_ref, rest_ref):
    size = own_field.shape[0] // 2
    core = chip_and_core()[1]
    for part, out in ((core, sent_ref), (1 - core, rest_ref)):
        rows = pl.ds(pl.multiple_of(part * size, size), size)
        out[:size, :] = own_field[rows, :]
        out[size:, :] = other_field[rows, :]


def last_kernel(image_ref, before_ref, *refs):
    count = len(refs) // 2 - 1
    fields, (out_ref, *rest_ref, factor_ref, spread_ref) = refs[:count], refs[count:]
    before = before_ref[...]
    image = dot_full(before, image_ref[...], NN)
    inner = dot_full(image, image, NT)
    if fields:
        rest_ref[0][...] = dot_full(fields[0][...], image_ref[...], NT)
    inverse_factor(inner, factor_ref, spread_ref)
    out_ref[...] = dot_full(factor_ref[...], before, NN)


def banded_kernel(blocks, basis_ref, field_ref, *refs):
    bands, (image_ref, before_ref, raw_ref, high_ref, low_ref, spread_ref) = refs[:-6], refs[-6:]
    group, core = chip_and_core()
    opposite = blocks // 2

    def store(row, column, part, mirror):
        rows = pl.ds(pl.multiple_of(row * BLOCK, BLOCK), BLOCK)
        columns = pl.ds(pl.multiple_of(column * BLOCK, BLOCK), BLOCK)
        high_ref[rows, columns], low_ref[rows, columns] = split(part)
        if mirror:
            high_ref[columns, rows], low_ref[columns, rows] = split(part.T)

    halves = {0: ((0, 0), (1, 0)), 1: ((2, 0), (1, 1)), 2: ((0, 1), (3, 0)), 3: ((2, 1), (3, 1))}
    half, band = bands[0].shape[0] // 2, bands[0].shape[1]
    for stacks, side in ((bands[:4], core), (bands[4:], 1 - core)):
        corners = {}
        for mask, places in halves.items():
            upper, lower = [stacks[number].at[half * part : half * (part + 1)] for number, part in places]
            row = 2 * jnp.bitwise_xor(group, mask) + side
            for k in range(opposite):
                inside = slice(BLOCK * k, BLOCK * (k + 1))
                part = jnp.concatenate([upper[:, inside], lower[: BLOCK - half, inside]], axis=0)
                store(row, lax.rem(row + k, blocks), part, k > 0)
            corners[mask] = jnp.concatenate(
                [lower[BLOCK - half :, BLOCK * i : BLOCK * (i + 1)] for i in range(band // BLOCK)], axis=0
            )
        for mask in (0, 1):
            row = 2 * jnp.bitwise_xor(group, mask) + side
            here, across = corners[mask], corners[mask ^ 2]
            near = row < opposite
            part = jnp.concatenate([jnp.where(near, here, across), jnp.where(near, across, here)], axis=0)
            row = lax.rem(row, opposite)
            store(row, row + opposite, part, True)
    sweeps(basis_ref, field_ref, image_ref, before_ref, raw_ref, high_ref, low_ref, spread_ref)


def whole_kernel(basis_ref, field_ref, gram_ref, image_ref, before_ref, raw_ref, high_ref, low_ref, spread_ref):
    high_ref[...], low_ref[...] = split(gram_ref[...])
    sweeps(basis_ref, field_ref, image_ref, before_ref, raw_ref, high_ref, low_ref, spread_ref)


def tail_kernel(cells_three, factor_ref, rest_ref, *refs):
    raw, (out_ref, own_ref, all_ref) = refs[:-3], refs[-3:]
    size = rest_ref.shape[0]
    cells_two = size // cells_three
    half = size // 2
    planes = len(raw)
    plane, core = lax.axis_index("narrow"), chip_and_core()[1]
    cores = dot_full(jnp.concatenate([part[...] for part in (rest_ref, *raw)], axis=0), factor_ref[...], NT)
    for k in range(planes + 1):
        part = cores[size * k : size * (k + 1)]
        if k < 2:
            place = pl.multiple_of((core if k else 1 - core) * half, half)
            own_ref[pl.ds(place, half), :] = part[:half]
            own_ref[pl.ds(size + place, half), :] = part[half:]
        if k > 0:
            place = pl.multiple_of(jnp.bitwise_xor(plane, k - 1) * half, half)
            all_ref[pl.ds(place, half), :] = part[:half]
            all_ref[pl.ds(planes * half + place, half), :] = part[half:]
    own, every = [], []
    for side in range(2):
        for k in range(cells_three):
            own.append(own_ref[pl.ds(size * side + k, cells_two, stride=cells_three), :])
            rows = planes * half // cells_three
            every.append(all_ref[pl.ds(planes * half * side + k, rows, stride=cells_three), :])
    out_ref[...] = dot_full(jnp.concatenate(own, axis=1), jnp.concatenate(every, axis=1), NT)


def call(kernel, outs, name, operands, scratch=(), order_only=(), flops=0, dtype=jnp.float32):
    shapes = [jax.ShapeDtypeStruct(shape, dtype) for shape in outs]
    touched = sum(operand.size for operand in operands) + sum(shape.size for shape in shapes)
    result = pl.pallas_call(
        kernel,
        out_shape=shapes,
        in_specs=[pl.BlockSpec(memory_space=pl.ANY)] * len(order_only) + [VMEM] * len(operands),
        out_specs=[VMEM] * len(shapes),
        scratch_shapes=list(scratch),
        compiler_params=pltpu.CompilerParams(vmem_limit_bytes=32 * 2**20),
        cost_estimate=pl.CostEstimate(flops=flops, bytes_accessed=4 * touched, transcendentals=0),
        name=name,
    )(*order_only, *operands)
    return result if len(outs) > 1 else result[0]


def swap(array, axis, mask):
    return lax.ppermute(array, axis, [(i, i ^ mask) for i in range(lax.axis_size(axis))])


def shards(field, start_block):
    cells_two, cells_three, order = field.shape
    rank = start_block.shape[1]
    narrow, wide = lax.axis_size("narrow"), lax.axis_size("wide")
    unfolded = field.reshape(cells_two * cells_three, order)
    cells = unfolded.shape[0]
    place = lax.axis_index("wide")
    spread = pltpu.VMEM((2 * PANEL * PANEL, rank), jnp.float32)

    def orthonormal_start(after):
        return call(
            start_kernel,
            [(rank, order)],
            "orth_start",
            [start_block],
            [pltpu.VMEM((rank, rank), jnp.float32), spread],
            order_only=[after],
            flops=10**9,
        )

    def last_factors(image, before, *fields):
        return call(
            last_kernel,
            [(rank, rank)] + [(cells, rank)] * len(fields),
            "last_factors",
            [image, before, *fields],
            [pltpu.VMEM((rank, rank), jnp.float32), spread],
            flops=10**9,
        )

    scratch = [
        pltpu.VMEM((order, order), jnp.bfloat16),
        pltpu.VMEM((order, order), jnp.bfloat16),
        spread,
    ]
    results = [(rank, order), (rank, rank), (cells, rank)]
    blocks = order // BLOCK
    if wide == blocks == 2 * narrow and narrow & (narrow - 1) == 0 and blocks // 2 % narrow == 0:
        groups = wide // 2
        band = order // 2
        half = (BLOCK + BLOCK // blocks) // 2
        extended = (cells, order + band - BLOCK)
        other = swap(unfolded, "wide", 1)
        own = call(split_kernel, [extended] * 2, "split_field", [unfolded], dtype=jnp.bfloat16)
        first_kept, first_sent, second_kept, second_sent = call(
            gram_kernel,
            [(2 * half, band)] * groups,
            "gram_band",
            [*own, other],
            [pltpu.VMEM((2 * cells, extended[1]), jnp.bfloat16)] * 2 + [pltpu.VMEM((BLOCK, BLOCK), jnp.float32)],
            flops=10**9,
        )
        first_got, second_got = swap(first_sent, "wide", 2), swap(second_sent, "wide", 4)
        basis = orthonormal_start(first_kept)
        sent_cells, rest_cells = call(halves_kernel, [(cells, order)] * 2, "half_cells", [unfolded, other])
        first, first_sent, second, second_sent = call(
            halve_kernel,
            [(half, band)] * 4,
            "sum_pairs",
            [first_kept, first_got, second_kept, second_got],
            order_only=[basis, sent_cells],
        )
        cuts = call(
            cut_kernel,
            [(2 * half, band // narrow)] * narrow,
            "sum_groups",
            [first, swap(first_sent, "wide", 4), second, swap(second_sent, "wide", 2)],
        )
        arrived = [swap(cuts[k], "narrow", k) for k in range(1, narrow)]
        piece = call(add_kernel, [(2 * half, band // narrow)], "sum_planes", [cuts[0], *arrived])
        arrived = [swap(piece, "narrow", k) for k in range(1, narrow)]
        first, second = call(
            join_kernel,
            [(half, band)] * 2,
            "join_planes",
            [piece, *arrived],
        )
        stacks = call(
            stack_kernel,
            [(2 * half, band)] * 2,
            "stack_pairs",
            [first, swap(first, "wide", 4), second, swap(second, "wide", 2)],
        )
        stacks = [*stacks, swap(stacks[0], "wide", 2), swap(stacks[1], "wide", 4)]
        bands = stacks + [swap(stack, "wide", 1) for stack in stacks]
        image, before, raw = call(
            functools.partial(banded_kernel, blocks),
            results,
            "sweeps",
            [basis, sent_cells, *bands],
            scratch,
        )
        raws = [raw] + [swap(raw, "narrow", k) for k in range(1, narrow)]
        factor, rest = last_factors(image, before, rest_cells)
        total = call(
            functools.partial(tail_kernel, cells_three),
            [(cells_two, narrow * cells_two // 2)],
            "core_pairs",
            [factor, rest, *raws],
            [pltpu.VMEM((2 * cells, rank), jnp.float32), pltpu.VMEM((narrow * cells, rank), jnp.float32)],
        )
        total = add_pairs([total] + [swap(total, "wide", 2 * k) for k in range(1, groups)])
        columns = narrow * cells_two // wide
        finished = lax.dynamic_slice_in_dim(total, place // 2 * columns, columns, 1)
    else:
        basis = orthonormal_start(start_block)
        gram = lax.dot_general(unfolded, unfolded, (((0,), (0,)), ((), ())), precision=HIGHEST)
        gram = lax.psum(gram, ("narrow", "wide"))
        image, before, raw = call(whole_kernel, results, "sweeps", [basis, unfolded, gram], scratch)
        core = lax.dot_general(raw, last_factors(image, before), NT, precision=HIGHEST)
        merged = core.reshape(cells_two, cells_three * rank)
        everyone = lax.all_gather(merged, "narrow", axis=0, tiled=True)
        part = lax.dot_general(merged, everyone, NT, precision=HIGHEST)
        finished = lax.psum_scatter(part, "wide", scatter_dimension=1, tiled=True)
    return finished / (rank * cells_three * wide)


def solution(mesh):
    return jax.shard_map(
        shards,
        mesh=mesh,
        in_specs=(P("narrow", "wide", None), P()),
        out_specs=P("narrow", "wide"),
        check_vma=False,
    )
```

```python
import functools
import jax
import jax.numpy as jnp
from jax import lax
from jax.experimental import pallas as pl
from jax.experimental.pallas import tpu as pltpu
from jax.sharding import PartitionSpec as P

ITERS = 4
BLOCK = 128
PANEL = 8
HIGHEST = lax.Precision.HIGHEST
NN = (((1,), (0,)), ((), ()))
NT = (((1,), (1,)), ((), ()))
VMEM = pl.BlockSpec(memory_space=pltpu.VMEM)


def split(values):
    high = values.astype(jnp.bfloat16)
    return high, (values - high.astype(jnp.float32)).astype(jnp.bfloat16)


def dot_bf16(left, right, dims):
    return lax.dot_general(left, right, dims, preferred_element_type=jnp.float32)


def dot_split(left, right, dims):
    (left_high, left_low), (right_high, right_low) = left, right
    return (
        dot_bf16(left_high, right_high, dims)
        + (dot_bf16(left_low, right_high, dims) + dot_bf16(left_high, right_low, dims))
    )


def dot_full(left, right, dims):
    return lax.dot_general(left, right, dims, precision=HIGHEST, preferred_element_type=jnp.float32)


def add_pairs(terms):
    terms = list(terms)
    while len(terms) > 1:
        pairs = [terms[i] + terms[i + 1] for i in range(0, len(terms) - 1, 2)]
        terms = pairs + terms[2 * len(pairs) :]
    return terms[0]


def inverse_factor(matrix, out_ref, scratch):
    order = matrix.shape[0]
    panels = order // PANEL
    tiles = [matrix[PANEL * i : PANEL * (i + 1), :] for i in range(panels)]
    lane = lax.broadcasted_iota(jnp.int32, (PANEL, order), 1)

    def full(part):
        return jnp.broadcast_to(part, (PANEL, order))

    for p in range(panels):
        tile, start = tiles[p], PANEL * p
        base = PANEL * PANEL * (p % 2)
        inside = (lane >= start) & (lane < start + PANEL)
        for c in range(PANEL):
            scratch[base + PANEL * c : base + PANEL * (c + 1), :] = full(tile[:, start + c : start + c + 1])
        pivot = {
            (r, c): full(scratch[base + PANEL * c + r : base + PANEL * c + r + 1, :])
            for c in range(PANEL)
            for r in range(c, PANEL)
        }
        rows = [
            jnp.where(inside, jnp.where(lane == start + c, 1.0, 0.0), full(tile[c : c + 1, :]))
            for c in range(PANEL)
        ]
        reciprocal, inverse = {}, {}
        for c in range(PANEL):
            reciprocal[c] = 1.0 / pivot[c, c]
            lower = {r: pivot[r, c] * reciprocal[c] for r in range(c + 1, PANEL)}
            for d in range(c + 1, PANEL):
                for r in range(d, PANEL):
                    if r == c + 1:
                        pivot[r, d] = pivot[r, d] - (pivot[r, c] * pivot[d, c]) * reciprocal[c]
                    else:
                        pivot[r, d] = pivot[r, d] - lower[r] * pivot[d, c]
            for r in range(c + 1, PANEL):
                rows[r] = rows[r] - lower[r] * rows[c]
                for k in range(c):
                    inverse[r, k] = inverse[r, k] - lower[r] * inverse[c, k]
                inverse[r, c] = -lower[r]
        for r in range(PANEL):
            done = jnp.where(lane < start + PANEL, rows[r], 0.0) * lax.rsqrt(pivot[r, r])
            out_ref[start + r : start + r + 1, :] = done[0:1, :]
        if p == panels - 1:
            break
        scaled = [rows[r] * reciprocal[r] for r in range(PANEL)]
        eliminate = []
        for c in range(PANEL):
            total = scaled[c]
            for r in range(c + 1, PANEL):
                total = total + inverse[r, c] * scaled[r]
            eliminate.append(total)
        for i in range(p + 1, panels):
            steps = [full(tiles[i][:, start + c : start + c + 1]) * eliminate[c] for c in range(PANEL)]
            tiles[i] = jnp.where(inside, 0.0, tiles[i]) - add_pairs(steps)


def start_kernel(after_ref, start_ref, out_ref, factor_ref, spread_ref):
    del after_ref
    rows = start_ref[...].T
    inverse_factor(dot_full(rows, rows, NT), factor_ref, spread_ref)
    out_ref[...] = dot_full(factor_ref[...], rows, NN)


def split_kernel(rows_ref, high_ref, low_ref):
    order = rows_ref.shape[1]
    extra = high_ref.shape[1] - order
    for target, values in zip((high_ref, low_ref), split(rows_ref[...])):
        target[:, 0:order] = values
        target[:, order : order + extra] = values[:, :extra]


def chip_and_core():
    place = lax.axis_index("wide")
    return place // 2, lax.rem(place, 2)


def gram_kernel(own_high, own_low, other_ref, *refs):
    outs, (high_ref, low_ref, corner_ref) = refs[:-3], refs[-3:]
    half, band = outs[0].shape[0] // 2, outs[0].shape[1]
    rows, order = other_ref.shape
    extra = high_ref.shape[1] - order
    for own, target, values in zip((own_high, own_low), (high_ref, low_ref), split(other_ref[...])):
        target[0:rows, :] = own[...]
        target[rows : 2 * rows, 0:order] = values
        target[rows : 2 * rows, order : order + extra] = values[:, :extra]
    group, core = chip_and_core()
    first_keep, first_send, second_keep, second_send = outs
    upper = [first_keep, first_send, first_keep, first_send]
    lower = [second_keep, second_keep, second_send, second_send]
    opposite = order // 2 // BLOCK

    def product(left_block, right_block, width):
        first = pl.multiple_of(left_block * BLOCK, BLOCK)
        second = pl.multiple_of(right_block * BLOCK, BLOCK)
        left = [ref[:, pl.ds(first, BLOCK)].astype(jnp.float32).T.astype(jnp.bfloat16) for ref in (high_ref, low_ref)]
        return dot_split(left, [ref[:, pl.ds(second, width)] for ref in (high_ref, low_ref)], NN)

    for k in range(len(outs)):
        block = 2 * jnp.bitwise_xor(group, k) + core
        corner = lax.rem(block, opposite)
        corner_ref[...] = product(corner, corner + opposite, BLOCK)
        part = corner_ref[pl.ds(pl.multiple_of(block // opposite * (BLOCK // 2), BLOCK // 2), BLOCK // 2), :]
        pieces = BLOCK * BLOCK // 2 // band
        part = jnp.concatenate([part[pieces * i : pieces * (i + 1), :] for i in range(band // BLOCK)], axis=1)
        whole = jnp.concatenate([product(block, block, band), part], axis=0)
        upper[k][half * (k // 2) : half * (k // 2 + 1), :] = whole[:half]
        lower[k][half * (k % 2) : half * (k % 2 + 1), :] = whole[half:]


def halve_kernel(after_ref, cells_ref, kept_first, got_first, kept_second, got_second, *outs):
    del after_ref, cells_ref
    half = kept_first.shape[0] // 2
    for kept, got, (own, send) in ((kept_first, got_first, outs[:2]), (kept_second, got_second, outs[2:])):
        own[...] = kept[:half, :] + got[:half, :]
        send[...] = kept[half:, :] + got[half:, :]


def cut_kernel(first, got_first, second, got_second, *outs):
    rows, columns = first.shape[0], outs[0].shape[1]
    plane = lax.axis_index("narrow")
    for k, out in enumerate(outs):
        piece = pl.ds(pl.multiple_of(jnp.bitwise_xor(plane, k) * columns, columns), columns)
        out[:rows, :] = first[:, piece] + got_first[:, piece]
        out[rows:, :] = second[:, piece] + got_second[:, piece]


def add_kernel(*refs):
    total = refs[0][...]
    for term in refs[1:-1]:
        total = total + term[...]
    refs[-1][...] = total


def join_kernel(*refs):
    pieces, (first, second) = refs[:-2], refs[-2:]
    rows, columns = first.shape[0], pieces[0].shape[1]
    plane = lax.axis_index("narrow")
    for k, piece in enumerate(pieces):
        place = pl.ds(pl.multiple_of(jnp.bitwise_xor(plane, k) * columns, columns), columns)
        first[:, place] = piece[:rows, :]
        second[:, place] = piece[rows:, :]


def stack_kernel(first, got_first, second, got_second, first_out, second_out):
    half = first.shape[0]
    for own, got, out in ((first, got_first, first_out), (second, got_second, second_out)):
        out[:half, :] = own[...]
        out[half:, :] = got[...]


def sweeps(basis_ref, field_ref, image_ref, factor_ref, raw_ref, high_ref, low_ref, spread_ref):
    def times_gram(rows):
        return dot_split(split(rows), (high_ref[...], low_ref[...]), NN)

    image = times_gram(basis_ref[...])
    for number in range(ITERS - 1):
        halves = split(image)
        inner = dot_split(halves, halves, NT) + dot_bf16(halves[1], halves[1], NT)
        following = times_gram(image)
        if number == ITERS - 2:
            image_ref[...] = following
            raw_ref[...] = dot_full(field_ref[...], following, NT)
        inverse_factor(inner, factor_ref, spread_ref)
        image = dot_full(factor_ref[...], following, NN)


def halves_kernel(own_field, other_field, sent_ref, rest_ref):
    size = own_field.shape[0] // 2
    core = chip_and_core()[1]
    for part, out in ((core, sent_ref), (1 - core, rest_ref)):
        rows = pl.ds(pl.multiple_of(part * size, size), size)
        out[:size, :] = own_field[rows, :]
        out[size:, :] = other_field[rows, :]


def last_kernel(image_ref, before_ref, *refs):
    count = len(refs) // 2 - 1
    fields, (out_ref, *rest_ref, factor_ref, spread_ref) = refs[:count], refs[count:]
    before = before_ref[...]
    image = dot_full(before, image_ref[...], NN)
    inner = dot_full(image, image, NT)
    if fields:
        rest_ref[0][...] = dot_full(fields[0][...], image_ref[...], NT)
    inverse_factor(inner, factor_ref, spread_ref)
    out_ref[...] = dot_full(factor_ref[...], before, NN)


def banded_kernel(blocks, basis_ref, field_ref, *refs):
    bands, (image_ref, before_ref, raw_ref, high_ref, low_ref, spread_ref) = refs[:-6], refs[-6:]
    group, core = chip_and_core()
    opposite = blocks // 2

    def store(row, column, part, mirror):
        rows = pl.ds(pl.multiple_of(row * BLOCK, BLOCK), BLOCK)
        columns = pl.ds(pl.multiple_of(column * BLOCK, BLOCK), BLOCK)
        high_ref[rows, columns], low_ref[rows, columns] = split(part)
        if mirror:
            high_ref[columns, rows], low_ref[columns, rows] = split(part.T)

    halves = {0: ((0, 0), (1, 0)), 1: ((2, 0), (1, 1)), 2: ((0, 1), (3, 0)), 3: ((2, 1), (3, 1))}
    half, band = bands[0].shape[0] // 2, bands[0].shape[1]
    for stacks, side in ((bands[:4], core), (bands[4:], 1 - core)):
        corners = {}
        for mask, places in halves.items():
            upper, lower = [stacks[number].at[half * part : half * (part + 1)] for number, part in places]
            row = 2 * jnp.bitwise_xor(group, mask) + side
            for k in range(opposite):
                inside = slice(BLOCK * k, BLOCK * (k + 1))
                part = jnp.concatenate([upper[:, inside], lower[: BLOCK - half, inside]], axis=0)
                store(row, lax.rem(row + k, blocks), part, k > 0)
            corners[mask] = jnp.concatenate(
                [lower[BLOCK - half :, BLOCK * i : BLOCK * (i + 1)] for i in range(band // BLOCK)], axis=0
            )
        for mask in (0, 1):
            row = 2 * jnp.bitwise_xor(group, mask) + side
            here, across = corners[mask], corners[mask ^ 2]
            near = row < opposite
            part = jnp.concatenate([jnp.where(near, here, across), jnp.where(near, across, here)], axis=0)
            row = lax.rem(row, opposite)
            store(row, row + opposite, part, True)
    sweeps(basis_ref, field_ref, image_ref, before_ref, raw_ref, high_ref, low_ref, spread_ref)


def whole_kernel(basis_ref, field_ref, gram_ref, image_ref, before_ref, raw_ref, high_ref, low_ref, spread_ref):
    high_ref[...], low_ref[...] = split(gram_ref[...])
    sweeps(basis_ref, field_ref, image_ref, before_ref, raw_ref, high_ref, low_ref, spread_ref)


def tail_kernel(cells_three, factor_ref, rest_ref, *refs):
    raw, (out_ref, own_ref, all_ref) = refs[:-3], refs[-3:]
    size = rest_ref.shape[0]
    cells_two = size // cells_three
    half = size // 2
    planes = len(raw)
    plane, core = lax.axis_index("narrow"), chip_and_core()[1]
    cores = dot_full(jnp.concatenate([part[...] for part in (rest_ref, *raw)], axis=0), factor_ref[...], NT)
    for k in range(planes + 1):
        part = cores[size * k : size * (k + 1)]
        if k < 2:
            place = pl.multiple_of((core if k else 1 - core) * half, half)
            own_ref[pl.ds(place, half), :] = part[:half]
            own_ref[pl.ds(size + place, half), :] = part[half:]
        if k > 0:
            place = pl.multiple_of(jnp.bitwise_xor(plane, k - 1) * half, half)
            all_ref[pl.ds(place, half), :] = part[:half]
            all_ref[pl.ds(planes * half + place, half), :] = part[half:]
    own, every = [], []
    for side in range(2):
        for k in range(cells_three):
            own.append(own_ref[pl.ds(size * side + k, cells_two, stride=cells_three), :])
            rows = planes * half // cells_three
            every.append(all_ref[pl.ds(planes * half * side + k, rows, stride=cells_three), :])
    out_ref[...] = dot_full(jnp.concatenate(own, axis=1), jnp.concatenate(every, axis=1), NT)


def call(kernel, outs, name, operands, scratch=(), order_only=(), flops=0, dtype=jnp.float32):
    shapes = [jax.ShapeDtypeStruct(shape, dtype) for shape in outs]
    touched = sum(operand.size for operand in operands) + sum(shape.size for shape in shapes)
    result = pl.pallas_call(
        kernel,
        out_shape=shapes,
        in_specs=[pl.BlockSpec(memory_space=pl.ANY)] * len(order_only) + [VMEM] * len(operands),
        out_specs=[VMEM] * len(shapes),
        scratch_shapes=list(scratch),
        compiler_params=pltpu.CompilerParams(vmem_limit_bytes=32 * 2**20),
        cost_estimate=pl.CostEstimate(flops=flops, bytes_accessed=4 * touched, transcendentals=0),
        name=name,
    )(*order_only, *operands)
    return result if len(outs) > 1 else result[0]


def swap(array, axis, mask):
    return lax.ppermute(array, axis, [(i, i ^ mask) for i in range(lax.axis_size(axis))])


def shards(field, start_block):
    cells_two, cells_three, order = field.shape
    rank = start_block.shape[1]
    narrow, wide = lax.axis_size("narrow"), lax.axis_size("wide")
    unfolded = field.reshape(cells_two * cells_three, order)
    cells = unfolded.shape[0]
    place = lax.axis_index("wide")
    spread = pltpu.VMEM((2 * PANEL * PANEL, rank), jnp.float32)

    def orthonormal_start(after):
        return call(
            start_kernel,
            [(rank, order)],
            "orth_start",
            [start_block],
            [pltpu.VMEM((rank, rank), jnp.float32), spread],
            order_only=[after],
            flops=10**9,
        )

    def last_factors(image, before, *fields):
        return call(
            last_kernel,
            [(rank, rank)] + [(cells, rank)] * len(fields),
            "last_factors",
            [image, before, *fields],
            [pltpu.VMEM((rank, rank), jnp.float32), spread],
            flops=10**9,
        )

    scratch = [
        pltpu.VMEM((order, order), jnp.bfloat16),
        pltpu.VMEM((order, order), jnp.bfloat16),
        spread,
    ]
    results = [(rank, order), (rank, rank), (cells, rank)]
    blocks = order // BLOCK
    if wide == blocks == 2 * narrow and narrow & (narrow - 1) == 0 and blocks // 2 % narrow == 0:
        groups = wide // 2
        band = order // 2
        half = (BLOCK + BLOCK // blocks) // 2
        extended = (cells, order + band - BLOCK)
        other = swap(unfolded, "wide", 1)
        own = call(split_kernel, [extended] * 2, "split_field", [unfolded], dtype=jnp.bfloat16)
        first_kept, first_sent, second_kept, second_sent = call(
            gram_kernel,
            [(2 * half, band)] * groups,
            "gram_band",
            [*own, other],
            [pltpu.VMEM((2 * cells, extended[1]), jnp.bfloat16)] * 2 + [pltpu.VMEM((BLOCK, BLOCK), jnp.float32)],
            flops=10**9,
        )
        first_got, second_got = swap(first_sent, "wide", 2), swap(second_sent, "wide", 4)
        basis = orthonormal_start(first_kept)
        sent_cells, rest_cells = call(halves_kernel, [(cells, order)] * 2, "half_cells", [unfolded, other])
        first, first_sent, second, second_sent = call(
            halve_kernel,
            [(half, band)] * 4,
            "sum_pairs",
            [first_kept, first_got, second_kept, second_got],
            order_only=[basis, sent_cells],
        )
        cuts = call(
            cut_kernel,
            [(2 * half, band // narrow)] * narrow,
            "sum_groups",
            [first, swap(first_sent, "wide", 4), second, swap(second_sent, "wide", 2)],
        )
        arrived = [swap(cuts[k], "narrow", k) for k in range(1, narrow)]
        piece = call(add_kernel, [(2 * half, band // narrow)], "sum_planes", [cuts[0], *arrived])
        arrived = [swap(piece, "narrow", k) for k in range(1, narrow)]
        first, second = call(
            join_kernel,
            [(half, band)] * 2,
            "join_planes",
            [piece, *arrived],
        )
        stacks = call(
            stack_kernel,
            [(2 * half, band)] * 2,
            "stack_pairs",
            [first, swap(first, "wide", 4), second, swap(second, "wide", 2)],
        )
        stacks = [*stacks, swap(stacks[0], "wide", 2), swap(stacks[1], "wide", 4)]
        bands = stacks + [swap(stack, "wide", 1) for stack in stacks]
        image, before, raw = call(
            functools.partial(banded_kernel, blocks),
            results,
            "sweeps",
            [basis, sent_cells, *bands],
            scratch,
        )
        raws = [raw] + [swap(raw, "narrow", k) for k in range(1, narrow)]
        factor, rest = last_factors(image, before, rest_cells)
        total = call(
            functools.partial(tail_kernel, cells_three),
            [(cells_two, narrow * cells_two // 2)],
            "core_pairs",
            [factor, rest, *raws],
            [pltpu.VMEM((2 * cells, rank), jnp.float32), pltpu.VMEM((narrow * cells, rank), jnp.float32)],
        )
        total = add_pairs([total] + [swap(total, "wide", 2 * k) for k in range(1, groups)])
        columns = narrow * cells_two // wide
        finished = lax.dynamic_slice_in_dim(total, place // 2 * columns, columns, 1)
    else:
        basis = orthonormal_start(start_block)
        gram = lax.dot_general(unfolded, unfolded, (((0,), (0,)), ((), ())), precision=HIGHEST)
        gram = lax.psum(gram, ("narrow", "wide"))
        image, before, raw = call(whole_kernel, results, "sweeps", [basis, unfolded, gram], scratch)
        core = lax.dot_general(raw, last_factors(image, before), NT, precision=HIGHEST)
        merged = core.reshape(cells_two, cells_three * rank)
        everyone = lax.all_gather(merged, "narrow", axis=0, tiled=True)
        part = lax.dot_general(merged, everyone, NT, precision=HIGHEST)
        finished = lax.psum_scatter(part, "wide", scatter_dimension=1, tiled=True)
    return finished / (rank * cells_three * wide)


def solution(mesh):
    return jax.shard_map(
        shards,
        mesh=mesh,
        in_specs=(P("narrow", "wide", None), P()),
        out_specs=P("narrow", "wide"),
        check_vma=False,
    )
```
